128 devices in a mesh: outer: 16 (over y, z_hi, core), inner: 8 (over x, z_lo).
Axes of the slice: x: 4, y: 4, z: 4 (z_hi: 2, z_lo: 2; z = z_hi * 2 + z_lo), core: 2. Of those that a mesh axis runs over, the one named last changes fastest.
Arguments:
- queries: bfloat16 [65536, 1024], P(('outer', 'inner')), may hold values from -5 to 5
- keys: bfloat16 [65536, 128], P(('outer', 'inner')), may hold values from -5 to 5
- values: bfloat16 [65536, 128], P(('outer', 'inner')), may hold values from -6 to 6
- grad_out: bfloat16 [65536, 1024], P(('outer', 'inner')), may hold values from -6 to 6
- doc_ids: int32 [65536], P(('outer', 'inner')), may hold values from 0 to 31, never falling along the last dimension, each value on 1 to 4096 neighbouring positions
Outputs:
- attn_out: bfloat16 [65536, 1024], P(('outer', 'inner'))
- grad_q: bfloat16 [65536, 1024], P(('outer', 'inner'))
- grad_k: bfloat16 [65536, 128], P(('outer', 'inner'))
- grad_v: bfloat16 [65536, 128], P(('outer', 'inner'))
The draws below stay inside these ranges and needn't reach their ends.
Inputs may be any that keep to these rules, and one draw needn't show every extreme that they name: doc_ids never falls along the positions; each document holds 1 to 4096 positions and one holds exactly 4096.
All inputs are finite; a program needn't handle non-finite values.
Results may differ from the reference program's by a relative error of at most 0.025.
Values may be sent and summed in bfloat16 or wider, within the bound.
No kernel may reach another device: no remote copies, remote signals or barrier semaphores. Data moves between devices by JAX's collectives and lax.ppermute only.
A program may use at most 128 MiB of HBM per device.

```python
import math
import jax
import jax.numpy as jnp
import numpy as np
from jax import lax

HEAD_DIM = 128
HEADS = 8
TILE = 128
TOKENS = 65536
MAXDOC = 4096
DOCS = 32


def draw_queries(key, part):
    key = jax.random.fold_in(key, 11)
    entries = jnp.clip(jax.random.normal(key, (TOKENS, HEADS, HEAD_DIM), jnp.float32), -4.5, 4.5)
    return entries.reshape(TOKENS, HEADS * HEAD_DIM).astype(jnp.bfloat16)


def draw_keys(key, part):
    key = jax.random.fold_in(key, 12)
    entries = jnp.clip(jax.random.normal(key, (TOKENS, HEAD_DIM), jnp.float32), -4.5, 4.5)
    return entries.astype(jnp.bfloat16)


def steps_of(own_key, dims, shards, low, high):
    level = 1.0
    for axis_at, parts in shards:
        steps = jax.random.uniform(jax.random.fold_in(jax.random.fold_in(own_key, 6), axis_at), (parts,), jnp.float32, low / len(shards), high / len(shards))
        level = level * jnp.repeat(jnp.exp(steps), dims[axis_at] // parts).reshape((-1,) + (1,) * (len(dims) - 1 - axis_at))
    return level


def length_profile(number_of, total, most, skew):
    portions = [(1 << 20) // math.isqrt(rank ** skew) + 1 for rank in range(2, number_of + 1)]
    spare, holding = total - most - (number_of - 1), [1] * (number_of - 1)
    while spare > 0:
        candidates = [i for i in range(number_of - 1) if holding[i] < most]
        pool, remaining = sum([portions[i] for i in candidates]), spare
        for i in candidates:
            extra = min(most - holding[i], max(1, remaining * portions[i] // pool), spare)
            holding[i] = holding[i] + extra
            spare = spare - extra
    return np.array([most] + holding)


def uneven_parts(own_key, number_of, total, reach, slope):
    if number_of == 2:
        one = jax.random.randint(own_key, (), max(1, total - reach), min(reach, total - 1) + 1)
        return jnp.stack([one, total - one])
    tallies = jnp.asarray(length_profile(number_of, total, reach, slope), jnp.int32)
    couples = (number_of - 1) // 2
    giver, taker = tallies[1:1 + 2 * couples:2], tallies[2:2 + 2 * couples:2]
    margin = jnp.minimum(giver - 1, reach - taker)
    moved = jax.random.randint(jax.random.fold_in(own_key, 1), (couples,), 0, 1 << 20) % (margin + 1)
    tallies = tallies.at[1:1 + 2 * couples:2].set(giver - moved).at[2:2 + 2 * couples:2].set(taker + moved)
    return tallies[jax.random.permutation(jax.random.fold_in(own_key, 2), number_of)]


def noise(rng, dims, spread, reach, cuts=(), held_as=jnp.bfloat16):
    result = spread * jax.random.normal(rng, dims, jnp.float32)
    if cuts:
        result = result * steps_of(rng, dims, cuts, -0.22, 0.18)
    return jnp.clip(result, -reach, reach).astype(held_as)


def setup_inputs(seed: int = 0) -> dict:
    arg_keys = jax.random.split(jax.random.key(seed), 6)
    queries = draw_queries(jax.random.fold_in(arg_keys[5], 71), 0)
    keys = draw_keys(jax.random.fold_in(arg_keys[5], 71), 0)
    values = noise(arg_keys[2], (TOKENS, HEAD_DIM), 1.0, 6.0, ((0, 128),))
    grad_out = noise(arg_keys[3], (TOKENS, HEADS * HEAD_DIM), 1.0, 6.0, ((0, 128),))
    doc_ids = jnp.searchsorted(jnp.cumsum(uneven_parts(arg_keys[4], DOCS, TOKENS, MAXDOC, 2)), jnp.arange(TOKENS), side="right").astype(jnp.int32)
    return {"queries": queries, "keys": keys, "values": values, "grad_out": grad_out, "doc_ids": doc_ids}


def round_trip(entries):
    return lax.optimization_barrier(entries.astype(jnp.bfloat16)).astype(jnp.float32)


def reference(queries, keys, values, grad_out, doc_ids):
    scale_value = HEAD_DIM ** -0.5
    window_len = MAXDOC + TILE
    zero_index = jnp.zeros((), jnp.int32)
    q_all = queries.reshape(TOKENS, HEADS, HEAD_DIM)
    d_all = grad_out.reshape(TOKENS, HEADS, HEAD_DIM)
    pad_keys = jnp.concatenate([jnp.zeros((window_len, HEAD_DIM), keys.dtype), keys], 0)
    pad_values = jnp.concatenate([jnp.zeros((window_len, HEAD_DIM), values.dtype), values], 0)
    pad_docs = jnp.concatenate([jnp.full((window_len,), -1, jnp.int32), doc_ids.astype(jnp.int32)], 0)
    key_offsets = jnp.arange(window_len, dtype=jnp.int32)
    row_offsets = jnp.arange(TILE, dtype=jnp.int32)
    doc_rows = doc_ids.astype(jnp.int32)

    def one_tile(carried, tile_index):
        key_accum, value_accum = carried
        tile_first = (tile_index * TILE).astype(jnp.int32)
        slot_start = (tile_first + TILE).astype(jnp.int32)
        q_tile = lax.dynamic_slice(q_all, (tile_first, zero_index, zero_index), (TILE, HEADS, HEAD_DIM)).astype(jnp.float32)
        d_tile = lax.dynamic_slice(d_all, (tile_first, zero_index, zero_index), (TILE, HEADS, HEAD_DIM)).astype(jnp.float32)
        key_window = lax.dynamic_slice(pad_keys, (slot_start, zero_index), (window_len, HEAD_DIM)).astype(jnp.float32)
        value_window = lax.dynamic_slice(pad_values, (slot_start, zero_index), (window_len, HEAD_DIM)).astype(jnp.float32)
        doc_window = lax.dynamic_slice(pad_docs, (slot_start,), (window_len,))
        row_docs = lax.dynamic_slice(doc_rows, (tile_first,), (TILE,))
        key_pos = tile_first + TILE - window_len + key_offsets
        row_pos = tile_first + row_offsets
        allowed = (doc_window[None, :] == row_docs[:, None]) & (key_pos[None, :] <= row_pos[:, None])
        scores = jnp.einsum("qhd,kd->hqk", q_tile, key_window) * scale_value
        scores = jnp.where(allowed[None], scores, -jnp.inf)
        row_top = jnp.max(scores, axis=2, keepdims=True)
        log_total = row_top + jnp.log(jnp.sum(jnp.exp(scores - row_top), axis=2, keepdims=True))
        probs = jnp.exp(scores - log_total)
        probs_b = round_trip(probs)
        out_tile = jnp.einsum("hqk,kd->qhd", probs_b, value_window).astype(jnp.bfloat16)
        row_delta = jnp.einsum("qhd,qhd->hq", d_tile, out_tile.astype(jnp.float32))
        dprobs = jnp.einsum("qhd,kd->hqk", d_tile, value_window)
        dscores = round_trip(probs * (dprobs - row_delta[..., None]))
        grad_tile = (scale_value * jnp.einsum("hqk,kd->qhd", dscores, key_window)).astype(jnp.bfloat16)
        key_part = jnp.einsum("hqk,qhd->kd", dscores, q_tile)
        value_part = jnp.einsum("hqk,qhd->kd", probs_b, d_tile)
        old_keys = lax.dynamic_slice(key_accum, (slot_start, zero_index), (window_len, HEAD_DIM))
        key_accum = lax.dynamic_update_slice(key_accum, old_keys + key_part, (slot_start, zero_index))
        old_values = lax.dynamic_slice(value_accum, (slot_start, zero_index), (window_len, HEAD_DIM))
        value_accum = lax.dynamic_update_slice(value_accum, old_values + value_part, (slot_start, zero_index))
        return (key_accum, value_accum), (out_tile, grad_tile)

    initial = (jnp.zeros((TOKENS + window_len, HEAD_DIM), jnp.float32), jnp.zeros((TOKENS + window_len, HEAD_DIM), jnp.float32))
    final, stacked = lax.scan(one_tile, initial, jnp.arange(TOKENS // TILE, dtype=jnp.int32))
    attn_out = stacked[0].reshape(TOKENS, HEADS * HEAD_DIM)
    grad_q = stacked[1].reshape(TOKENS, HEADS * HEAD_DIM)
    grad_k = (scale_value * final[0][window_len:]).astype(jnp.bfloat16)
    grad_v = final[1][window_len:].astype(jnp.bfloat16)
    return (attn_out, grad_q, grad_k, grad_v)
```

```python
import jax
import jax.numpy as jnp
from jax import lax
from jax.experimental import pallas as pl
from jax.experimental.pallas import tpu as pltpu
from jax.sharding import PartitionSpec as P

LOG2E = 1.4426950408889634
LOW = -1e30
LANES = 128
DOC_ROWS = 16
f32 = jnp.float32
bf16 = jnp.bfloat16
NN = (((1,), (0,)), ((), ()))
NT = (((1,), (1,)), ((), ()))


def dot(a, b, dims=NN):
    return lax.dot_general(a, b, dims, preferred_element_type=f32)


def attention_kernel(
    heads,
    inner_ref,
    near_ref,
    own_ref,
    q_ref,
    do_ref,
    out_ref,
    dq_ref,
    dnear_ref,
    down_ref,
    s_ref,
    p_ref,
    k_ref,
    v_ref,
    m_ref,
    acc_ref,
    dqa_ref,
    dk_ref,
    dv_ref,
    doc_ref,
    rowdoc_ref,
    edge_ref,
):
    rows, width = q_ref.shape
    dim = width // heads
    blocks = near_ref.shape[0] + 1
    last = blocks - 1
    tiles = rows // LANES
    scale = dim ** (-0.5)
    inner = inner_ref[0]

    for w in range(blocks):
        if w < last:
            block = near_ref[lax.rem(inner + w, last)]
        else:
            block = own_ref[...]
        k_ref[w] = block[0:rows, 0:dim]
        v_ref[w, :, 0:dim] = block[0:rows, dim : 2 * dim]
        v_ref[w, :, dim : 2 * dim] = jnp.ones((rows, dim), bf16)
        docs = block[rows : rows + DOC_ROWS, :].astype(f32)
        for t in range(tiles):
            part = docs[t // 2 : t // 2 + 1, (t % 2) * LANES : (t % 2 + 1) * LANES]
            doc_ref[w, 0:1, t * LANES : (t + 1) * LANES] = part
        edge_ref[w] = jnp.max(doc_ref[w, 0:1, 0:1]).astype(jnp.int32)
        edge_ref[blocks + w] = jnp.max(doc_ref[w, 0:1, rows - 1 : rows]).astype(jnp.int32)
    first = edge_ref[last]
    whole = edge_ref[blocks + last] == first
    lo = jnp.int32(0)
    for w in range(last):
        lo = lo + jnp.where(edge_ref[blocks + w] == first, 0, 1)
    rowdoc_ref[...] = jnp.broadcast_to(doc_ref[last, 0:1, :], (LANES, rows)).T
    dk_ref[...] = jnp.zeros_like(dk_ref)
    dv_ref[...] = jnp.zeros_like(dv_ref)

    def tile(x, t):
        return x[:, t * LANES : (t + 1) * LANES]

    def head_step(h, carry):
        cols = pl.ds(pl.multiple_of(h * dim, dim), dim)
        q = q_ref[:, cols]
        do = do_ref[:, cols]
        m_ref[...] = jnp.full_like(m_ref, LOW)

        def keep(w, s):
            s_ref[w] = s
            m = m_ref[...]
            for t in range(tiles):
                m = jnp.maximum(m, tile(s, t))
            m_ref[...] = m

        def same_doc(w, t):
            return rowdoc_ref[...] == doc_ref[w, 0:1, t * LANES : (t + 1) * LANES]

        def score_step(w, c):
            clean = jnp.logical_and(whole, edge_ref[w] == first)

            @pl.when(clean)
            def _():
                keep(w, dot(q, k_ref[w], NT))

            @pl.when(jnp.logical_not(clean))
            def _():
                s = dot(q, k_ref[w], NT)
                parts = [jnp.where(same_doc(w, t), tile(s, t), LOW) for t in range(tiles)]
                keep(w, jnp.concatenate(parts, 1))

            return c

        lax.fori_loop(lo, last, score_step, 0)
        s = dot(q, k_ref[last], NT)
        row = lax.broadcasted_iota(jnp.int32, (rows, LANES), 0)
        col = lax.broadcasted_iota(jnp.int32, (rows, LANES), 1)
        parts = [
            jnp.where(same_doc(last, t) & (col + t * LANES <= row), tile(s, t), LOW)
            for t in range(tiles)
        ]
        keep(last, jnp.concatenate(parts, 1))
        top = jnp.max(m_ref[...], axis=1, keepdims=True) * (scale * LOG2E)
        m_ref[...] = jnp.broadcast_to(top, (rows, LANES))
        acc_ref[...] = jnp.zeros_like(acc_ref)

        def value_step(w, c):
            s = s_ref[w]
            m = m_ref[...]
            parts = [jnp.exp2(tile(s, t) * (scale * LOG2E) - m) for t in range(tiles)]
            p = jnp.concatenate(parts, 1).astype(bf16)
            p_ref[w] = p
            acc_ref[...] += dot(p, v_ref[w])
            return c

        lax.fori_loop(lo, blocks, value_step, 0)
        inv = 1.0 / acc_ref[:, dim : 2 * dim]
        out = (acc_ref[:, 0:dim] * inv).astype(bf16)
        out_ref[:, cols] = out
        dof = do.astype(f32)
        delta = jnp.sum(dof * out.astype(f32), axis=1, keepdims=True)
        delta = jnp.broadcast_to(delta, (rows, LANES))
        d1 = delta.astype(bf16).astype(f32)
        d2 = (delta - d1).astype(bf16).astype(f32)
        d3 = delta - d1 - d2
        minus = jnp.where(col == 0, -d1, jnp.where(col == 1, -d2, jnp.where(col == 2, -d3, 0.0)))
        do_delta = jnp.concatenate([do, minus.astype(bf16)], 1)
        q_inv = (q.astype(f32) * inv).T.astype(bf16)
        do_inv = (dof * inv).T.astype(bf16)
        dqa_ref[...] = jnp.zeros_like(dqa_ref)

        def grad_step(w, c):
            p = p_ref[w]
            dp = dot(do_delta, v_ref[w], NT)
            ds = (p.astype(f32) * dp).astype(bf16)
            dqa_ref[...] += dot(ds, k_ref[w])
            dk_ref[w] += dot(q_inv, ds)
            dv_ref[w] += dot(do_inv, p)
            return c

        lax.fori_loop(lo, blocks, grad_step, 0)
        dq_ref[:, cols] = (dqa_ref[...] * inv * scale).astype(bf16)
        return carry

    lax.fori_loop(0, heads, head_step, 0)
    for w in range(blocks):
        dk = dk_ref[w].T * scale
        dv = dv_ref[w].T
        if w < last:
            peer = lax.rem(inner + w, last)
            dnear_ref[peer, :, 0:dim] = dk.astype(bf16)
            dnear_ref[peer, :, dim : 2 * dim] = dv.astype(bf16)
        else:
            down_ref[:, 0:dim] = dk
            down_ref[:, dim : 2 * dim] = dv


def attention(inner_pos, near, own, queries, grad_out, dim):
    rows, width = queries.shape
    blocks = near.shape[0] + 1
    vmem = pl.BlockSpec(memory_space=pltpu.VMEM)
    return pl.pallas_call(
        lambda *refs: attention_kernel(width // dim, *refs),
        out_shape=[
            jax.ShapeDtypeStruct((rows, width), bf16),
            jax.ShapeDtypeStruct((rows, width), bf16),
            jax.ShapeDtypeStruct((blocks - 1, rows, 2 * dim), bf16),
            jax.ShapeDtypeStruct((rows, 2 * dim), f32),
        ],
        in_specs=[pl.BlockSpec(memory_space=pltpu.SMEM), vmem, vmem, vmem, vmem],
        out_specs=[vmem] * 4,
        scratch_shapes=[
            pltpu.VMEM((blocks, rows, rows), f32),
            pltpu.VMEM((blocks, rows, rows), bf16),
            pltpu.VMEM((blocks, rows, dim), bf16),
            pltpu.VMEM((blocks, rows, 2 * dim), bf16),
            pltpu.VMEM((rows, LANES), f32),
            pltpu.VMEM((rows, 2 * dim), f32),
            pltpu.VMEM((rows, dim), f32),
            pltpu.VMEM((blocks, dim, rows), f32),
            pltpu.VMEM((blocks, dim, rows), f32),
            pltpu.VMEM((blocks, 8, rows), f32),
            pltpu.VMEM((rows, LANES), f32),
            pltpu.SMEM((2 * blocks,), jnp.int32),
        ],
        compiler_params=pltpu.CompilerParams(vmem_limit_bytes=60 * 1024 * 1024),
        name="attention",
    )(inner_pos, near, own, queries, grad_out)


def shift_groups(block, by):
    count = lax.axis_size("outer")
    return lax.ppermute(block, "outer", [(i, (i + by) % count) for i in range(count)])


def on_device(queries, keys, values, grad_out, doc_ids):
    rows, dim = keys.shape
    inner_count = lax.axis_size("inner")
    inner_pos = lax.axis_index("inner")
    peers = jnp.arange(inner_count, dtype=jnp.int32)[:, None, None]
    docs = doc_ids.astype(bf16).reshape(rows // (2 * dim), 2 * dim)
    docs = jnp.pad(docs, ((0, DOC_ROWS - docs.shape[0]), (0, 0)))
    own = jnp.concatenate([jnp.concatenate([keys, values], 1), docs], 0)
    behind = shift_groups(own, 1)
    to_send = jnp.where(peers > inner_pos, own[None], behind[None])
    near = lax.all_to_all(to_send, "inner", 0, 0, tiled=True)
    attn_out, grad_q, near_grads, own_grads = attention(
        inner_pos.astype(jnp.int32).reshape(1), near, own, queries, grad_out, dim
    )
    terms = lax.all_to_all(near_grads, "inner", 0, 0, tiled=True).astype(f32)
    ahead = peers > inner_pos
    back = jnp.sum(jnp.where(ahead, 0.0, terms), 0).astype(bf16)
    back = shift_groups(back, -1)
    grads = own_grads + jnp.sum(jnp.where(ahead, terms, 0.0), 0) + back.astype(f32)
    grads = grads.astype(bf16)
    return (attn_out, grad_q, grads[:, :dim], grads[:, dim:])


def solution(mesh):
    rows = P(("outer", "inner"), None)
    return jax.shard_map(
        on_device,
        mesh=mesh,
        in_specs=(rows, rows, rows, rows, P(("outer", "inner"))),
        out_specs=(rows, rows, rows, rows),
        check_vma=False,
    )
```

```python
import jax
import jax.numpy as jnp
from jax import lax
from jax.experimental import pallas as pl
from jax.experimental.pallas import tpu as pltpu
from jax.sharding import PartitionSpec as P

LOG2E = 1.4426950408889634
LOW = -1e30
HEADROOM = 64.0
LANES = 128
DOC_ROWS = 16
STACK = 4
VMEM_BYTES = 56 * 1024 * 1024
f32 = jnp.float32
bf16 = jnp.bfloat16
NN = (((1,), (0,)), ((), ()))
NT = (((1,), (1,)), ((), ()))


def dot(a, b, dims=NN):
    return lax.dot_general(a, b, dims, preferred_element_type=f32)


def tile(x, t):
    return x[:, t * LANES : (t + 1) * LANES]


def attention_kernel(near_count, heads, *refs):
    refs = list(refs)
    near = [refs.pop(0) for _ in range(near_count)]
    own, q_ref, do_ref, inner_ref, out_ref, dq_ref, dnear, down = [refs.pop(0) for _ in range(8)]
    p_ref, k_ref, v_ref, m_ref, peak_ref, acc_ref, dqa_ref, dk_ref, dv_ref, doc_ref, rowdoc_ref = refs
    rows, width = q_ref.shape
    dim = width // heads
    last = near_count
    blocks = near_count + 1
    tiles = rows // LANES
    stacked = STACK * rows
    scale = dim ** (-0.5)

    for w, ref in enumerate(near + [own]):
        k_ref[w] = ref[0:rows, 0:dim]
        v_ref[w, :, 0:dim] = ref[0:rows, dim : 2 * dim]
        v_ref[w, :, dim : 2 * dim] = jnp.ones((rows, dim), bf16)
        docs = ref[rows : rows + DOC_ROWS, :].astype(f32)
        for t in range(tiles):
            part = docs[t // 2 : t // 2 + 1, (t % 2) * LANES : (t % 2 + 1) * LANES]
            doc_ref[w, 0:1, t * LANES : (t + 1) * LANES] = part
    first = jnp.broadcast_to(doc_ref[last, 0:1, 0:1], (1, LANES))
    spare = jnp.zeros((1, LANES), f32)
    for w in range(last):
        end = jnp.broadcast_to(doc_ref[w, 0:1, rows - 1 : rows], (1, LANES))
        spare = spare + jnp.where(end == first, 0.0, 1.0)
    lo = jnp.max(spare).astype(jnp.int32)
    spread = jnp.broadcast_to(doc_ref[last, 0:1, :], (LANES, rows)).T
    rowdoc_ref[...] = jnp.concatenate([spread] * STACK, 0)
    dk_ref[...] = jnp.zeros_like(dk_ref)
    dv_ref[...] = jnp.zeros_like(dv_ref)
    row = lax.rem(lax.broadcasted_iota(jnp.int32, (stacked, LANES), 0), rows)
    col = lax.broadcasted_iota(jnp.int32, (stacked, LANES), 1)

    def scores(q, w, own_block):
        s = dot(q, k_ref[w], NT)
        parts = []
        for t in range(tiles):
            mask = rowdoc_ref[...] == doc_ref[w, 0:1, t * LANES : (t + 1) * LANES]
            if own_block:
                mask = mask & (col + t * LANES <= row)
            parts.append(jnp.where(mask, tile(s, t), LOW))
        return parts

    def attend(w, parts):
        m = m_ref[...]
        p = jnp.concatenate([jnp.exp2(s * (scale * LOG2E) - m) for s in parts], 1).astype(bf16)
        p_ref[w] = p
        acc_ref[...] += dot(p, v_ref[w])

    def row_max(x):
        return jnp.broadcast_to(jnp.max(x, axis=1, keepdims=True), x.shape)

    def step(at, carry):
        columns = [
            pl.ds(pl.multiple_of((at * STACK + i) * dim, dim), dim) for i in range(STACK)
        ]
        q = jnp.concatenate([q_ref[:, c] for c in columns], 0)
        do = jnp.concatenate([do_ref[:, c] for c in columns], 0)
        acc_ref[...] = jnp.zeros_like(acc_ref)
        parts = scores(q, last, True)
        top = parts[0]
        for s in parts[1:]:
            top = jnp.maximum(top, s)
        m_ref[...] = row_max(top) * (scale * LOG2E)
        attend(last, parts)
        peak_ref[...] = jnp.full_like(peak_ref, LOW)

        def near_block(w, c):
            parts = scores(q, w, False)
            peak = peak_ref[...]
            for s in parts:
                peak = jnp.maximum(peak, s)
            peak_ref[...] = peak
            attend(w, parts)
            return c

        lax.fori_loop(lo, last, near_block, 0)
        excess = peak_ref[...] * (scale * LOG2E) - m_ref[...]

        @pl.when(jnp.max(excess) > HEADROOM)
        def _():
            m_ref[...] = jnp.maximum(m_ref[...], row_max(peak_ref[...]) * (scale * LOG2E))
            acc_ref[...] = jnp.zeros_like(acc_ref)

            def again(w, c):
                attend(w, scores(q, w, False))
                return c

            lax.fori_loop(lo, last, again, 0)
            attend(last, scores(q, last, True))

        inv = 1.0 / acc_ref[:, dim : 2 * dim]
        out = (acc_ref[:, 0:dim] * inv).astype(bf16)
        dof = do.astype(f32)
        delta = jnp.sum(dof * out.astype(f32), axis=1, keepdims=True)
        m_ref[...] = jnp.broadcast_to(delta, m_ref.shape)
        q_inv = (q.astype(f32) * inv).astype(bf16).T
        do_inv = (dof * inv).astype(bf16).T
        dqa_ref[...] = jnp.zeros_like(dqa_ref)

        def grad_block(w, c):
            dp = dot(do, v_ref[w, :, 0:dim], NT)
            delta = m_ref[...]
            p = p_ref[w]
            parts = [
                (tile(p, t).astype(f32) * (tile(dp, t) - delta)).astype(bf16)
                for t in range(tiles)
            ]
            ds = jnp.concatenate(parts, 1)
            dqa_ref[...] += dot(ds, k_ref[w])
            dk_ref[w] += dot(q_inv, ds)
            dv_ref[w] += dot(do_inv, p)
            return c

        lax.fori_loop(lo, blocks, grad_block, 0)
        dq = (dqa_ref[...] * inv * scale).astype(bf16)
        for i, c in enumerate(columns):
            out_ref[:, c] = out[i * rows : (i + 1) * rows]
            dq_ref[:, c] = dq[i * rows : (i + 1) * rows]
        return carry

    lax.fori_loop(0, heads // STACK, step, 0)
    for w in range(near_count):
        peer = lax.rem(inner_ref[0] + w, near_count)
        dnear[peer, 0:dim] = (dk_ref[w] * scale).astype(bf16)
        dnear[peer, dim : 2 * dim] = dv_ref[w].astype(bf16)
    down[0:dim] = dk_ref[last] * scale
    down[dim : 2 * dim] = dv_ref[last]


def attention(near, own, queries, grad_out, inner_pos, dim):
    rows, width = queries.shape
    count = len(near)
    stacked = STACK * rows
    vmem = pl.BlockSpec(memory_space=pltpu.VMEM)
    wide = jax.ShapeDtypeStruct((rows, width), bf16)
    outs = [wide, wide, pltpu.VMEM((count, 2 * dim, rows), bf16)]
    outs += [jax.ShapeDtypeStruct((2 * dim, rows), f32)]
    return pl.pallas_call(
        lambda *refs: attention_kernel(count, width // dim, *refs),
        out_shape=outs,
        in_specs=[vmem] * (count + 3) + [pl.BlockSpec(memory_space=pltpu.SMEM)],
        out_specs=[vmem] * len(outs),
        scratch_shapes=[
            pltpu.VMEM((count + 1, stacked, rows), bf16),
            pltpu.VMEM((count + 1, rows, dim), bf16),
            pltpu.VMEM((count + 1, rows, 2 * dim), bf16),
            pltpu.VMEM((stacked, LANES), f32),
            pltpu.VMEM((stacked, LANES), f32),
            pltpu.VMEM((stacked, 2 * dim), f32),
            pltpu.VMEM((stacked, dim), f32),
            pltpu.VMEM((count + 1, dim, rows), f32),
            pltpu.VMEM((count + 1, dim, rows), f32),
            pltpu.VMEM((count + 1, 8, rows), f32),
            pltpu.VMEM((stacked, LANES), f32),
        ],
        compiler_params=pltpu.CompilerParams(vmem_limit_bytes=VMEM_BYTES),
        name="attention",
    )(*near, own, queries, grad_out, inner_pos)


def shift(block, axes, by):
    count = lax.axis_size(axes)
    return lax.ppermute(block, axes, [(i, (i + by) % count) for i in range(count)])


def on_device(queries, keys, values, grad_out, doc_ids):
    rows, dim = keys.shape
    reach = lax.axis_size("inner")
    inner_pos = lax.axis_index("inner").astype(jnp.int32)
    docs = doc_ids.astype(bf16).reshape(rows // (2 * dim), 2 * dim)
    docs = jnp.pad(docs, ((0, DOC_ROWS - docs.shape[0]), (0, 0)))
    own = jnp.concatenate([jnp.concatenate([keys, values], 1), docs], 0)
    near = [shift(own, ("outer", "inner"), by) for by in range(reach, 0, -1)]
    attn_out, grad_q, near_grads, own_grads = attention(
        near, own, queries, grad_out, inner_pos.reshape(1), dim
    )
    terms = lax.all_to_all(near_grads, "inner", 0, 0, tiled=True).astype(f32)
    peers = jnp.arange(reach, dtype=jnp.int32)[:, None, None]
    ahead = peers > inner_pos
    back = jnp.sum(jnp.where(ahead, 0.0, terms), 0).astype(bf16)
    back = shift(back, "outer", -1)
    grads = own_grads + jnp.sum(jnp.where(ahead, terms, 0.0), 0) + back.astype(f32)
    grads = grads.T.astype(bf16)
    return (attn_out, grad_q, grads[:, :dim], grads[:, dim:])


def solution(mesh):
    rows = P(("outer", "inner"), None)
    return jax.shard_map(
        on_device,
        mesh=mesh,
        in_specs=(rows, rows, rows, rows, P(("outer", "inner"))),
        out_specs=(rows, rows, rows, rows),
        check_vma=False,
    )
```

```python
import jax
import jax.numpy as jnp
from jax import lax
from jax.experimental import pallas as pl
from jax.experimental.pallas import tpu as pltpu
from jax.sharding import PartitionSpec as P

LOG2E = 1.4426950408889634
LOW = -1e30
HEADROOM = 64.0
LANES = 128
DOC_ROWS = 16
STACK = 4
FAR = 5
VMEM_BYTES = 40 * 1024 * 1024
f32 = jnp.float32
bf16 = jnp.bfloat16
NN = (((1,), (0,)), ((), ()))
NT = (((1,), (1,)), ((), ()))


def dot(a, b, dims=NN):
    return lax.dot_general(a, b, dims, preferred_element_type=f32)


def tile(x, t):
    return x[:, t * LANES : (t + 1) * LANES]


def spread(column, like):
    return jnp.broadcast_to(column, like.shape)


class Window:
    def __init__(self, near, own, heads, q_ref, k_ref, v_ref, doc_ref, rowdoc_ref):
        rows, width = q_ref.shape
        self.rows, self.dim = rows, width // heads
        self.last = len(near)
        self.scale = self.dim ** (-0.5)
        self.k_ref, self.doc_ref, self.rowdoc_ref = k_ref, doc_ref, rowdoc_ref
        for w, ref in enumerate(near + [own]):
            if w < k_ref.shape[0]:
                k_ref[w] = ref[0:rows, 0 : self.dim]
                v_ref[w, :, 0 : self.dim] = ref[0:rows, self.dim : 2 * self.dim]
                if v_ref.shape[2] > self.dim:
                    v_ref[w, :, self.dim : 2 * self.dim] = jnp.ones((rows, self.dim), bf16)
            docs = ref[rows : rows + DOC_ROWS, :].astype(f32)
            for t in range(rows // LANES):
                part = docs[t // 2 : t // 2 + 1, (t % 2) * LANES : (t % 2 + 1) * LANES]
                doc_ref[w, 0:1, t * LANES : (t + 1) * LANES] = part
        first = jnp.broadcast_to(doc_ref[self.last, 0:1, 0:1], (1, LANES))
        spare = jnp.zeros((1, LANES), f32)
        for w in range(self.last):
            end = jnp.broadcast_to(doc_ref[w, 0:1, rows - 1 : rows], (1, LANES))
            spare = spare + jnp.where(end == first, 0.0, 1.0)
        self.lo = jnp.max(spare).astype(jnp.int32)
        row_docs = jnp.broadcast_to(doc_ref[self.last, 0:1, :], (LANES, rows)).T
        rowdoc_ref[...] = jnp.concatenate([row_docs] * STACK, 0)

    def masks(self, w, own_block):
        shape = self.rowdoc_ref.shape
        masks = []
        for t in range(self.rows // LANES):
            mask = self.rowdoc_ref[...] == self.doc_ref[w, 0:1, t * LANES : (t + 1) * LANES]
            if own_block:
                row = lax.rem(lax.broadcasted_iota(jnp.int32, shape, 0), self.rows)
                col = lax.broadcasted_iota(jnp.int32, shape, 1) + t * LANES
                mask = mask & (col <= row)
            masks.append(mask)
        return masks

    def scores(self, q, w, own_block):
        s = dot(q, self.k_ref[w], NT)
        return [
            jnp.where(mask, tile(s, t), LOW) for t, mask in enumerate(self.masks(w, own_block))
        ]

    def columns(self, at):
        return [
            pl.ds(pl.multiple_of((at * STACK + i) * self.dim, self.dim), self.dim)
            for i in range(STACK)
        ]

    def stacked_rows(self, at):
        count = STACK * self.rows
        return pl.ds(pl.multiple_of(at * count, count), count)

    def stack(self, ref, at):
        return jnp.concatenate([ref[:, c] for c in self.columns(at)], 0)

    def unstack(self, ref, at, value):
        for i, c in enumerate(self.columns(at)):
            ref[:, c] = value[i * self.rows : (i + 1) * self.rows]


def attend_near(window, q, own_block, m_ref, peak_ref, acc_ref, v_ref, p_ref, refill):
    scale = window.scale * LOG2E

    def attend(w, parts):
        m = m_ref[...]
        p = jnp.concatenate([jnp.exp2(s * scale - m) for s in parts], 1).astype(bf16)
        if p_ref is not None:
            p_ref[w] = p
        acc_ref[...] += dot(p, v_ref[w])

    if own_block:
        parts = window.scores(q, window.last, True)
        top = parts[0]
        for s in parts[1:]:
            top = jnp.maximum(top, s)
        refill(spread(jnp.max(top, axis=1, keepdims=True), top) * scale)
        attend(window.last, parts)
    else:
        refill(None)
    peak_ref[...] = jnp.full_like(peak_ref, LOW)

    def block(w, c):
        parts = window.scores(q, w, False)
        peak = peak_ref[...]
        for s in parts:
            peak = jnp.maximum(peak, s)
        peak_ref[...] = peak
        attend(w, parts)
        return c

    lax.fori_loop(window.lo, window.last, block, 0)
    excess = peak_ref[...] * scale - m_ref[...]

    @pl.when(jnp.max(excess) > HEADROOM)
    def _():
        peak = peak_ref[...]
        refill(jnp.maximum(m_ref[...], spread(jnp.max(peak, axis=1, keepdims=True), peak) * scale))

        def again(w, c):
            attend(w, window.scores(q, w, False))
            return c

        lax.fori_loop(window.lo, window.last, again, 0)
        if own_block:
            attend(window.last, window.scores(q, window.last, True))


def start_kernel(count, heads, *refs):
    refs = list(refs)
    near = [refs.pop(0) for _ in range(count)]
    own, q_ref, acc_out, m_out, l_out = [refs.pop(0) for _ in range(5)]
    k_ref, v_ref, m_ref, peak_ref, acc_ref, doc_ref, rowdoc_ref = refs
    window = Window(near, own, heads, q_ref, k_ref, v_ref, doc_ref, rowdoc_ref)
    dim = window.dim

    def step(at, carry):
        def refill(top):
            m_ref[...] = top
            acc_ref[...] = jnp.zeros_like(acc_ref)

        q = window.stack(q_ref, at)
        attend_near(window, q, True, m_ref, peak_ref, acc_ref, v_ref, None, refill)
        window.unstack(acc_out, at, acc_ref[:, 0:dim])
        m_out[window.stacked_rows(at)] = m_ref[...]
        l_out[window.stacked_rows(at)] = acc_ref[:, dim : 2 * dim]
        return carry

    lax.fori_loop(0, heads // STACK, step, 0)


def far_kernel(count, heads, *refs):
    refs = list(refs)
    near = [refs.pop(0) for _ in range(count)]
    own, q_ref, do_ref, acc_in, m_in, l_in = [refs.pop(0) for _ in range(6)]
    out_ref, dq_ref, log_ref, delta_ref = [refs.pop(0) for _ in range(4)]
    dnear = [refs.pop(0) for _ in range(count)]
    k_ref, v_ref, m_ref, peak_ref, acc_ref, doc_ref, rowdoc_ref, p_ref, dqa_ref, dk_ref, dv_ref = (
        refs
    )
    window = Window(near, own, heads, q_ref, k_ref, v_ref, doc_ref, rowdoc_ref)
    dim, tiles = window.dim, window.rows // LANES
    dk_ref[...] = jnp.zeros_like(dk_ref)
    dv_ref[...] = jnp.zeros_like(dv_ref)

    def step(at, carry):
        here = window.stacked_rows(at)

        def refill(top):
            old = m_in[here]
            m_ref[...] = old if top is None else top
            shrink = 1.0 if top is None else jnp.exp2(old - top)
            acc_ref[:, 0:dim] = window.stack(acc_in, at) * shrink
            acc_ref[:, dim : 2 * dim] = l_in[here] * shrink

        q = window.stack(q_ref, at)
        do = window.stack(do_ref, at)
        attend_near(window, q, False, m_ref, peak_ref, acc_ref, v_ref, p_ref, refill)
        total = acc_ref[:, dim : 2 * dim]
        inv = 1.0 / total
        out = (acc_ref[:, 0:dim] * inv).astype(bf16)
        dof = do.astype(f32)
        delta = jnp.sum(dof * out.astype(f32), axis=1, keepdims=True)
        log_ref[here] = m_ref[...] + jnp.log(total) * LOG2E
        delta_ref[here] = spread(delta, total)
        q_inv = (q.astype(f32) * inv).astype(bf16).T
        do_inv = (dof * inv).astype(bf16).T
        dqa_ref[...] = jnp.zeros_like(dqa_ref)

        def grad_block(w, c):
            dp = dot(do, v_ref[w, :, 0:dim], NT)
            delta = delta_ref[here]
            p = p_ref[w]
            parts = [
                (tile(p, t).astype(f32) * (tile(dp, t) - delta)).astype(bf16)
                for t in range(tiles)
            ]
            ds = jnp.concatenate(parts, 1)
            dqa_ref[...] += dot(ds, k_ref[w])
            dk_ref[w] += dot(q_inv, ds)
            dv_ref[w] += dot(do_inv, p)
            return c

        lax.fori_loop(window.lo, window.last, grad_block, 0)
        window.unstack(out_ref, at, out)
        window.unstack(dq_ref, at, dqa_ref[...] * inv)
        return carry

    lax.fori_loop(0, heads // STACK, step, 0)
    for w in range(count):
        dnear[w][0:dim] = (dk_ref[w] * window.scale).astype(bf16)
        dnear[w][dim : 2 * dim] = dv_ref[w].astype(bf16)


def near_kernel(count, heads, *refs):
    refs = list(refs)
    near = [refs.pop(0) for _ in range(count)]
    own, q_ref, do_ref, dq_in, log_ref, delta_ref = [refs.pop(0) for _ in range(6)]
    dq_ref = refs.pop(0)
    dnear = [refs.pop(0) for _ in range(count)]
    down, k_ref, v_ref, doc_ref, rowdoc_ref, dqa_ref, dk_ref, dv_ref = refs
    window = Window(near, own, heads, q_ref, k_ref, v_ref, doc_ref, rowdoc_ref)
    dim, scale = window.dim, window.scale
    dk_ref[...] = jnp.zeros_like(dk_ref)
    dv_ref[...] = jnp.zeros_like(dv_ref)

    def step(at, carry):
        here = window.stacked_rows(at)
        q = window.stack(q_ref, at)
        do = window.stack(do_ref, at)
        q_t = q.T
        do_t = do.T
        dqa_ref[...] = window.stack(dq_in, at)

        def grad_block(w, own_block):
            s = dot(q, k_ref[w], NT)
            dp = dot(do, v_ref[w], NT)
            top = log_ref[here]
            delta = delta_ref[here]
            probs = []
            dscores = []
            for t, mask in enumerate(window.masks(w, own_block)):
                p = jnp.where(mask, jnp.exp2(tile(s, t) * (scale * LOG2E) - top), 0.0)
                probs.append(p.astype(bf16))
                dscores.append((p * (tile(dp, t) - delta)).astype(bf16))
            ds = jnp.concatenate(dscores, 1)
            dqa_ref[...] += dot(ds, k_ref[w])
            dk_ref[w] += dot(q_t, ds)
            dv_ref[w] += dot(do_t, jnp.concatenate(probs, 1))

        def near_block(w, c):
            grad_block(w, False)
            return c

        lax.fori_loop(window.lo, window.last, near_block, 0)
        grad_block(window.last, True)
        window.unstack(dq_ref, at, (dqa_ref[...] * scale).astype(bf16))
        return carry

    lax.fori_loop(0, heads // STACK, step, 0)
    for w in range(count):
        dnear[w][0:dim] = (dk_ref[w] * scale).astype(bf16)
        dnear[w][dim : 2 * dim] = dv_ref[w].astype(bf16)
    down[0:dim] = dk_ref[count] * scale
    down[dim : 2 * dim] = dv_ref[count]


def call(kernel, near, args, outs, scratch, heads, name):
    args = [pltpu.with_memory_space_constraint(a, pltpu.VMEM) for a in [*near, *args]]
    vmem = pl.BlockSpec(memory_space=pltpu.VMEM)
    return pl.pallas_call(
        lambda *refs: kernel(len(near), heads, *refs),
        out_shape=outs,
        in_specs=[vmem] * len(args),
        out_specs=[vmem] * len(outs),
        scratch_shapes=scratch,
        compiler_params=pltpu.CompilerParams(vmem_limit_bytes=VMEM_BYTES),
        name=name,
    )(*args)


def attention_start(near, own, queries, dim):
    rows, width = queries.shape
    heads, blocks, stacked = width // dim, len(near) + 1, STACK * rows
    by_head = pltpu.VMEM((heads * rows, LANES), f32)
    outs = [pltpu.VMEM((rows, width), f32), by_head, by_head]
    scratch = [
        pltpu.VMEM((blocks, rows, dim), bf16),
        pltpu.VMEM((blocks, rows, 2 * dim), bf16),
        pltpu.VMEM((stacked, LANES), f32),
        pltpu.VMEM((stacked, LANES), f32),
        pltpu.VMEM((stacked, 2 * dim), f32),
        pltpu.VMEM((blocks, 8, rows), f32),
        pltpu.VMEM((stacked, LANES), f32),
    ]
    return call(start_kernel, near, (own, queries), outs, scratch, heads, "forward_near")


def attention_far(near, own, queries, grad_out, state, dim):
    rows, width = queries.shape
    heads, blocks, stacked = width // dim, len(near), STACK * rows
    by_head = pltpu.VMEM((heads * rows, LANES), f32)
    outs = [jax.ShapeDtypeStruct((rows, width), bf16), pltpu.VMEM((rows, width), f32)]
    outs += [by_head, by_head] + [pltpu.VMEM((2 * dim, rows), bf16)] * blocks
    scratch = [
        pltpu.VMEM((blocks, rows, dim), bf16),
        pltpu.VMEM((blocks, rows, 2 * dim), bf16),
        pltpu.VMEM((stacked, LANES), f32),
        pltpu.VMEM((stacked, LANES), f32),
        pltpu.VMEM((stacked, 2 * dim), f32),
        pltpu.VMEM((blocks + 1, 8, rows), f32),
        pltpu.VMEM((stacked, LANES), f32),
        pltpu.VMEM((blocks, stacked, rows), bf16),
        pltpu.VMEM((stacked, dim), f32),
        pltpu.VMEM((blocks, dim, rows), f32),
        pltpu.VMEM((blocks, dim, rows), f32),
    ]
    args = (own, queries, grad_out, *state)
    return call(far_kernel, near, args, outs, scratch, heads, "attention_far")


def attention_near(near, own, queries, grad_out, dq, log_total, delta, dim):
    rows, width = queries.shape
    heads, blocks, stacked = width // dim, len(near) + 1, STACK * rows
    outs = [jax.ShapeDtypeStruct((rows, width), bf16)]
    outs += [pltpu.VMEM((2 * dim, rows), bf16)] * len(near)
    outs += [jax.ShapeDtypeStruct((2 * dim, rows), f32)]
    scratch = [
        pltpu.VMEM((blocks, rows, dim), bf16),
        pltpu.VMEM((blocks, rows, dim), bf16),
        pltpu.VMEM((blocks, 8, rows), f32),
        pltpu.VMEM((stacked, LANES), f32),
        pltpu.VMEM((stacked, dim), f32),
        pltpu.VMEM((blocks, dim, rows), f32),
        pltpu.VMEM((blocks, dim, rows), f32),
    ]
    args = (own, queries, grad_out, dq, log_total, delta)
    return call(near_kernel, near, args, outs, scratch, heads, "backward_near")


def shift(block, by):
    axes = ("outer", "inner")
    count = lax.axis_size(axes)
    return lax.ppermute(block, axes, [(i, (i + by) % count) for i in range(count)])


def on_device(queries, keys, values, grad_out, doc_ids):
    rows, dim = keys.shape
    reach = lax.axis_size("inner")
    docs = doc_ids.astype(bf16).reshape(rows // (2 * dim), 2 * dim)
    docs = jnp.pad(docs, ((0, DOC_ROWS - docs.shape[0]), (0, 0)))
    own = jnp.concatenate([jnp.concatenate([keys, values], 1), docs], 0)
    near = [shift(own, reach - i) for i in range(FAR, reach)]
    later, near = lax.optimization_barrier((own, near))
    far = [shift(later, reach - i) for i in range(FAR)]
    state = attention_start(near, own, queries, dim)
    attn_out, dq, log_total, delta, *far_grads = attention_far(
        far, own, queries, grad_out, state, dim
    )
    far_terms = [shift(g, i - reach) for i, g in enumerate(far_grads)]
    grad_q, *near_grads, grads = attention_near(
        near, own, queries, grad_out, dq, log_total, delta, dim
    )
    far_sum = sum(term.astype(f32) for term in far_terms)
    far_sum, near_grads = lax.optimization_barrier((far_sum, near_grads))
    near_terms = [shift(g, i + FAR - reach) for i, g in enumerate(near_grads)]
    grads = grads + far_sum + sum(term.astype(f32) for term in near_terms)
    grads = grads.T.astype(bf16)
    return (attn_out, grad_q, grads[:, :dim], grads[:, dim:])


def solution(mesh):
    rows = P(("outer", "inner"), None)
    return jax.shard_map(
        on_device,
        mesh=mesh,
        in_specs=(rows, rows, rows, rows, P(("outer", "inner"))),
        out_specs=(rows, rows, rows, rows),
        check_vma=False,
    )
```

```python
from functools import partial

import jax
import jax.numpy as jnp
from jax import lax
from jax.experimental import pallas as pl
from jax.experimental.pallas import tpu as pltpu
from jax.sharding import PartitionSpec as P

LOG2E = 1.4426950408889634
LOW = -1e30
HEADROOM = 64.0
LANES = 128
DOC_ROWS = 16
STACK = 4
FAR = 5
PARTS = (4, 3, 1)
VMEM_BYTES = 40 * 1024 * 1024
f32 = jnp.float32
bf16 = jnp.bfloat16
NN = (((1,), (0,)), ((), ()))
NT = (((1,), (1,)), ((), ()))


def dot(a, b, dims=NN):
    return lax.dot_general(a, b, dims, preferred_element_type=f32)


def tile(x, t):
    return x[:, t * LANES : (t + 1) * LANES]


def spread(column, like):
    return jnp.broadcast_to(column, like.shape)


class Window:
    def __init__(self, near, own, heads, q_ref, k_ref, v_ref, doc_ref, rowdoc_ref):
        rows, width = q_ref.shape
        self.rows, self.dim = rows, width // heads
        self.last = len(near)
        self.scale = self.dim ** (-0.5)
        self.k_ref, self.doc_ref, self.rowdoc_ref = k_ref, doc_ref, rowdoc_ref
        for w, ref in enumerate(near + [own]):
            if w < k_ref.shape[0]:
                k_ref[w] = ref[0:rows, 0 : self.dim]
                v_ref[w, :, 0 : self.dim] = ref[0:rows, self.dim : 2 * self.dim]
                if v_ref.shape[2] > self.dim:
                    v_ref[w, :, self.dim : 2 * self.dim] = jnp.ones((rows, self.dim), bf16)
            docs = ref[rows : rows + DOC_ROWS, :].astype(f32)
            for t in range(rows // LANES):
                part = docs[t // 2 : t // 2 + 1, (t % 2) * LANES : (t % 2 + 1) * LANES]
                doc_ref[w, 0:1, t * LANES : (t + 1) * LANES] = part
        first = jnp.broadcast_to(doc_ref[self.last, 0:1, 0:1], (1, LANES))
        spare = jnp.zeros((1, LANES), f32)
        for w in range(self.last):
            end = jnp.broadcast_to(doc_ref[w, 0:1, rows - 1 : rows], (1, LANES))
            spare = spare + jnp.where(end == first, 0.0, 1.0)
        self.lo = jnp.max(spare).astype(jnp.int32)
        row_docs = jnp.broadcast_to(doc_ref[self.last, 0:1, :], (LANES, rows)).T
        rowdoc_ref[...] = jnp.concatenate([row_docs] * STACK, 0)

    def masks(self, w, own_block):
        shape = self.rowdoc_ref.shape
        masks = []
        for t in range(self.rows // LANES):
            mask = self.rowdoc_ref[...] == self.doc_ref[w, 0:1, t * LANES : (t + 1) * LANES]
            if own_block:
                row = lax.rem(lax.broadcasted_iota(jnp.int32, shape, 0), self.rows)
                col = lax.broadcasted_iota(jnp.int32, shape, 1) + t * LANES
                mask = mask & (col <= row)
            masks.append(mask)
        return masks

    def scores(self, q, w, own_block):
        s = dot(q, self.k_ref[w], NT)
        return [
            jnp.where(mask, tile(s, t), LOW) for t, mask in enumerate(self.masks(w, own_block))
        ]

    def columns(self, at):
        return [
            pl.ds(pl.multiple_of((at * STACK + i) * self.dim, self.dim), self.dim)
            for i in range(STACK)
        ]

    def stacked_rows(self, at):
        count = STACK * self.rows
        return pl.ds(pl.multiple_of(at * count, count), count)

    def stack(self, ref, at):
        return jnp.concatenate([ref[:, c] for c in self.columns(at)], 0)

    def unstack(self, ref, at, value):
        for i, c in enumerate(self.columns(at)):
            ref[:, c] = value[i * self.rows : (i + 1) * self.rows]


def attend_near(window, q, own_block, m_ref, peak_ref, acc_ref, v_ref, p_ref, refill):
    scale = window.scale * LOG2E

    def attend(w, parts):
        m = m_ref[...]
        p = jnp.concatenate([jnp.exp2(s * scale - m) for s in parts], 1).astype(bf16)
        if p_ref is not None:
            p_ref[w] = p
        acc_ref[...] += dot(p, v_ref[w])

    if own_block:
        parts = window.scores(q, window.last, True)
        top = parts[0]
        for s in parts[1:]:
            top = jnp.maximum(top, s)
        refill(spread(jnp.max(top, axis=1, keepdims=True), top) * scale)
        attend(window.last, parts)
    else:
        refill(None)
    peak_ref[...] = jnp.full_like(peak_ref, LOW)

    def block(w, c):
        parts = window.scores(q, w, False)
        peak = peak_ref[...]
        for s in parts:
            peak = jnp.maximum(peak, s)
        peak_ref[...] = peak
        attend(w, parts)
        return c

    lax.fori_loop(window.lo, window.last, block, 0)
    excess = peak_ref[...] * scale - m_ref[...]

    @pl.when(jnp.max(excess) > HEADROOM)
    def _():
        peak = peak_ref[...]
        refill(jnp.maximum(m_ref[...], spread(jnp.max(peak, axis=1, keepdims=True), peak) * scale))

        def again(w, c):
            attend(w, window.scores(q, w, False))
            return c

        lax.fori_loop(window.lo, window.last, again, 0)
        if own_block:
            attend(window.last, window.scores(q, window.last, True))


def start_kernel(count, heads, *refs):
    refs = list(refs)
    near = [refs.pop(0) for _ in range(count)]
    own, q_ref, acc_out, m_out, l_out = [refs.pop(0) for _ in range(5)]
    k_ref, v_ref, m_ref, peak_ref, acc_ref, doc_ref, rowdoc_ref = refs
    window = Window(near, own, heads, q_ref, k_ref, v_ref, doc_ref, rowdoc_ref)
    dim = window.dim

    def step(at, carry):
        def refill(top):
            m_ref[...] = top
            acc_ref[...] = jnp.zeros_like(acc_ref)

        q = window.stack(q_ref, at)
        attend_near(window, q, True, m_ref, peak_ref, acc_ref, v_ref, None, refill)
        window.unstack(acc_out, at, acc_ref[:, 0:dim])
        m_out[window.stacked_rows(at)] = m_ref[...]
        l_out[window.stacked_rows(at)] = acc_ref[:, dim : 2 * dim]
        return carry

    lax.fori_loop(0, heads // STACK, step, 0)


def far_kernel(count, heads, *refs):
    back = PARTS[0]
    refs = list(refs)
    near = [refs.pop(0) for _ in range(count)]
    own, q_ref, do_ref, acc_in, m_in, l_in = [refs.pop(0) for _ in range(6)]
    out_ref, dq_ref, log_ref, delta_ref = [refs.pop(0) for _ in range(4)]
    dnear = [refs.pop(0) for _ in range(back)]
    k_ref, v_ref, m_ref, peak_ref, acc_ref, doc_ref, rowdoc_ref, p_ref, dqa_ref, dk_ref, dv_ref = (
        refs
    )
    window = Window(near, own, heads, q_ref, k_ref, v_ref, doc_ref, rowdoc_ref)
    dim, tiles = window.dim, window.rows // LANES
    dk_ref[...] = jnp.zeros_like(dk_ref)
    dv_ref[...] = jnp.zeros_like(dv_ref)

    def step(at, carry):
        here = window.stacked_rows(at)

        def refill(top):
            old = m_in[here]
            m_ref[...] = old if top is None else top
            shrink = 1.0 if top is None else jnp.exp2(old - top)
            acc_ref[:, 0:dim] = window.stack(acc_in, at) * shrink
            acc_ref[:, dim : 2 * dim] = l_in[here] * shrink

        q = window.stack(q_ref, at)
        do = window.stack(do_ref, at)
        attend_near(window, q, False, m_ref, peak_ref, acc_ref, v_ref, p_ref, refill)
        total = acc_ref[:, dim : 2 * dim]
        inv = 1.0 / total
        out = (acc_ref[:, 0:dim] * inv).astype(bf16)
        dof = do.astype(f32)
        delta = jnp.sum(dof * out.astype(f32), axis=1, keepdims=True)
        log_ref[here] = m_ref[...] + jnp.log(total) * LOG2E
        delta_ref[here] = spread(delta, total)
        q_inv = (q.astype(f32) * inv).astype(bf16).T
        do_inv = (dof * inv).astype(bf16).T
        dqa_ref[...] = jnp.zeros_like(dqa_ref)

        def grad_block(w, c):
            dp = dot(do, v_ref[w, :, 0:dim], NT)
            delta = delta_ref[here]
            p = p_ref[w]
            parts = [
                (tile(p, t).astype(f32) * (tile(dp, t) - delta)).astype(bf16)
                for t in range(tiles)
            ]
            ds = jnp.concatenate(parts, 1)
            dqa_ref[...] += dot(ds, k_ref[w])
            dk_ref[w] += dot(q_inv, ds)
            dv_ref[w] += dot(do_inv, p)
            return c

        lax.fori_loop(window.lo, back, grad_block, 0)
        window.unstack(out_ref, at, out)
        window.unstack(dq_ref, at, dqa_ref[...] * inv)
        return carry

    lax.fori_loop(0, heads // STACK, step, 0)
    for w in range(back):
        dnear[w][0:dim] = (dk_ref[w] * window.scale).astype(bf16)
        dnear[w][dim : 2 * dim] = dv_ref[w].astype(bf16)


def back_kernel(final, count, heads, *refs):
    refs = list(refs)
    near = [refs.pop(0) for _ in range(count)]
    own, q_ref, do_ref, dq_in, log_ref, delta_ref = [refs.pop(0) for _ in range(6)]
    dq_ref = refs.pop(0)
    dnear = [refs.pop(0) for _ in range(count)]
    down = refs.pop(0) if final else None
    k_ref, v_ref, doc_ref, rowdoc_ref, dqa_ref, dk_ref, dv_ref = refs
    window = Window(near, own, heads, q_ref, k_ref, v_ref, doc_ref, rowdoc_ref)
    dim, scale = window.dim, window.scale
    dk_ref[...] = jnp.zeros_like(dk_ref)
    dv_ref[...] = jnp.zeros_like(dv_ref)

    def step(at, carry):
        here = window.stacked_rows(at)
        q = window.stack(q_ref, at)
        do = window.stack(do_ref, at)
        q_t = q.T
        do_t = do.T
        dqa_ref[...] = window.stack(dq_in, at)

        def grad_block(w, own_block):
            s = dot(q, k_ref[w], NT)
            dp = dot(do, v_ref[w], NT)
            top = log_ref[here]
            delta = delta_ref[here]
            probs = []
            dscores = []
            for t, mask in enumerate(window.masks(w, own_block)):
                p = jnp.where(mask, jnp.exp2(tile(s, t) * (scale * LOG2E) - top), 0.0)
                probs.append(p.astype(bf16))
                dscores.append((p * (tile(dp, t) - delta)).astype(bf16))
            ds = jnp.concatenate(dscores, 1)
            dqa_ref[...] += dot(ds, k_ref[w])
            dk_ref[w] += dot(q_t, ds)
            dv_ref[w] += dot(do_t, jnp.concatenate(probs, 1))

        def near_block(w, c):
            grad_block(w, False)
            return c

        lax.fori_loop(window.lo, window.last, near_block, 0)
        if final:
            grad_block(window.last, True)
            window.unstack(dq_ref, at, (dqa_ref[...] * scale).astype(bf16))
        else:
            window.unstack(dq_ref, at, dqa_ref[...])
        return carry

    lax.fori_loop(0, heads // STACK, step, 0)
    for w in range(count):
        dnear[w][0:dim] = (dk_ref[w] * scale).astype(bf16)
        dnear[w][dim : 2 * dim] = dv_ref[w].astype(bf16)
    if final:
        down[0:dim] = dk_ref[count] * scale
        down[dim : 2 * dim] = dv_ref[count]


def sum_kernel(down, *refs):
    *terms, dk_ref, dv_ref = refs
    total = down[...]
    for term in terms:
        total = total + term[...].astype(f32)
    dim = dk_ref.shape[1]
    dk_ref[...] = total[0:dim].T.astype(bf16)
    dv_ref[...] = total[dim : 2 * dim].T.astype(bf16)


def call(kernel, near, args, outs, scratch, heads, name):
    args = [pltpu.with_memory_space_constraint(a, pltpu.VMEM) for a in [*near, *args]]
    vmem = pl.BlockSpec(memory_space=pltpu.VMEM)
    return pl.pallas_call(
        lambda *refs: kernel(len(near), heads, *refs),
        out_shape=outs,
        in_specs=[vmem] * len(args),
        out_specs=[vmem] * len(outs),
        scratch_shapes=scratch,
        compiler_params=pltpu.CompilerParams(vmem_limit_bytes=VMEM_BYTES),
        name=name,
    )(*args)


def attention_start(near, own, queries, dim):
    rows, width = queries.shape
    heads, blocks, stacked = width // dim, len(near) + 1, STACK * rows
    by_head = pltpu.VMEM((heads * rows, LANES), f32)
    outs = [pltpu.VMEM((rows, width), f32), by_head, by_head]
    scratch = [
        pltpu.VMEM((blocks, rows, dim), bf16),
        pltpu.VMEM((blocks, rows, 2 * dim), bf16),
        pltpu.VMEM((stacked, LANES), f32),
        pltpu.VMEM((stacked, LANES), f32),
        pltpu.VMEM((stacked, 2 * dim), f32),
        pltpu.VMEM((blocks, 8, rows), f32),
        pltpu.VMEM((stacked, LANES), f32),
    ]
    return call(start_kernel, near, (own, queries), outs, scratch, heads, "forward_near")


def attention_far(near, own, queries, grad_out, state, dim):
    rows, width = queries.shape
    heads, blocks, stacked = width // dim, len(near), STACK * rows
    by_head = pltpu.VMEM((heads * rows, LANES), f32)
    outs = [jax.ShapeDtypeStruct((rows, width), bf16), pltpu.VMEM((rows, width), f32)]
    outs += [by_head, by_head] + [pltpu.VMEM((2 * dim, rows), bf16)] * PARTS[0]
    scratch = [
        pltpu.VMEM((blocks, rows, dim), bf16),
        pltpu.VMEM((blocks, rows, 2 * dim), bf16),
        pltpu.VMEM((stacked, LANES), f32),
        pltpu.VMEM((stacked, LANES), f32),
        pltpu.VMEM((stacked, 2 * dim), f32),
        pltpu.VMEM((blocks + 1, 8, rows), f32),
        pltpu.VMEM((stacked, LANES), f32),
        pltpu.VMEM((blocks, stacked, rows), bf16),
        pltpu.VMEM((stacked, dim), f32),
        pltpu.VMEM((PARTS[0], dim, rows), f32),
        pltpu.VMEM((PARTS[0], dim, rows), f32),
    ]
    args = (own, queries, grad_out, *state)
    return call(far_kernel, near, args, outs, scratch, heads, "attention_far")


def attention_back(final, near, own, queries, grad_out, dq, log_total, delta, dim):
    rows, width = queries.shape
    heads, blocks, stacked = width // dim, len(near) + int(final), STACK * rows
    if final:
        outs = [jax.ShapeDtypeStruct((rows, width), bf16)]
    else:
        outs = [pltpu.VMEM((rows, width), f32)]
    outs += [pltpu.VMEM((2 * dim, rows), bf16)] * len(near)
    if final:
        outs += [pltpu.VMEM((2 * dim, rows), f32)]
    scratch = [
        pltpu.VMEM((blocks, rows, dim), bf16),
        pltpu.VMEM((blocks, rows, dim), bf16),
        pltpu.VMEM((len(near) + 1, 8, rows), f32),
        pltpu.VMEM((stacked, LANES), f32),
        pltpu.VMEM((stacked, dim), f32),
        pltpu.VMEM((blocks, dim, rows), f32),
        pltpu.VMEM((blocks, dim, rows), f32),
    ]
    args = (own, queries, grad_out, dq, log_total, delta)
    name = "backward_final" if final else "backward_mid"
    return call(partial(back_kernel, final), near, args, outs, scratch, heads, name)


def sum_terms(down, terms, dim):
    rows = down.shape[1]
    out = jax.ShapeDtypeStruct((rows, dim), bf16)
    return call(
        lambda count, heads, *refs: sum_kernel(*refs), [down], terms, [out, out], [], 1, "sum_terms"
    )


def shift(block, by):
    axes = ("outer", "inner")
    count = lax.axis_size(axes)
    return lax.ppermute(block, axes, [(i, (i + by) % count) for i in range(count)])


def on_device(queries, keys, values, grad_out, doc_ids):
    rows, dim = keys.shape
    reach = lax.axis_size("inner")
    docs = doc_ids.astype(bf16).reshape(rows // (2 * dim), 2 * dim)
    docs = jnp.pad(docs, ((0, DOC_ROWS - docs.shape[0]), (0, 0)))
    own = jnp.concatenate([jnp.concatenate([keys, values], 1), docs], 0)
    behind = [shift(own, reach - i) for i in range(reach)]
    state = attention_start(behind[FAR:], own, queries, dim)
    attn_out, dq, log_total, delta, *grads = attention_far(
        behind[:FAR], own, queries, grad_out, state, dim
    )
    terms = [shift(g, i - reach) for i, g in enumerate(grads)]
    done = PARTS[0]
    for part in PARTS[1:]:
        final = done + part == reach
        dq, *grads = attention_back(
            final, behind[done : done + part], own, queries, grad_out, dq, log_total, delta, dim
        )
        terms, grads = lax.optimization_barrier((terms, grads))
        terms += [shift(g, done + i - reach) for i, g in enumerate(grads[:part])]
        done += part
    grad_k, grad_v = sum_terms(grads[-1], terms, dim)
    return (attn_out, dq, grad_k, grad_v)


def solution(mesh):
    rows = P(("outer", "inner"), None)
    return jax.shard_map(
        on_device,
        mesh=mesh,
        in_specs=(rows, rows, rows, rows, P(("outer", "inner"))),
        out_specs=(rows, rows, rows, rows),
        check_vma=False,
    )
```

```python
from functools import partial

import jax
import jax.numpy as jnp
from jax import lax
from jax.experimental import pallas as pl
from jax.experimental.pallas import tpu as pltpu
from jax.sharding import PartitionSpec as P

LOG2E = 1.4426950408889634
LOW = -1e30
HEADROOM = 64.0
LANES = 128
DOC_ROWS = 16
STACK = 4
FAR = 5
PARTS = (5, 3, 0)
VMEM_BYTES = 34 * 1024 * 1024
f32 = jnp.float32
bf16 = jnp.bfloat16
NN = (((1,), (0,)), ((), ()))
NT = (((1,), (1,)), ((), ()))


def dot(a, b, dims=NN):
    return lax.dot_general(a, b, dims, preferred_element_type=f32)


def tile(x, t):
    return x[:, t * LANES : (t + 1) * LANES]


def spread(column, like):
    return jnp.broadcast_to(column, like.shape)


class Window:
    def __init__(self, near, own, heads, q_ref, k_ref, v_ref, doc_ref, rowdoc_ref):
        rows, width = q_ref.shape
        self.rows, self.dim = rows, width // heads
        self.last = len(near)
        self.scale = self.dim ** (-0.5)
        self.k_ref, self.doc_ref, self.rowdoc_ref = k_ref, doc_ref, rowdoc_ref
        for w, ref in enumerate(near + [own]):
            if w < k_ref.shape[0]:
                k_ref[w] = ref[0:rows, 0 : self.dim]
                v_ref[w, :, 0 : self.dim] = ref[0:rows, self.dim : 2 * self.dim]
                if v_ref.shape[2] > self.dim:
                    v_ref[w, :, self.dim : 2 * self.dim] = jnp.ones((rows, self.dim), bf16)
            docs = ref[rows : rows + DOC_ROWS, :].astype(f32)
            for t in range(rows // LANES):
                part = docs[t // 2 : t // 2 + 1, (t % 2) * LANES : (t % 2 + 1) * LANES]
                doc_ref[w, 0:1, t * LANES : (t + 1) * LANES] = part
        first = jnp.broadcast_to(doc_ref[self.last, 0:1, 0:1], (1, LANES))
        spare = jnp.zeros((1, LANES), f32)
        for w in range(self.last):
            end = jnp.broadcast_to(doc_ref[w, 0:1, rows - 1 : rows], (1, LANES))
            spare = spare + jnp.where(end == first, 0.0, 1.0)
        self.lo = jnp.max(spare).astype(jnp.int32)
        row_docs = jnp.broadcast_to(doc_ref[self.last, 0:1, :], (LANES, rows)).T
        rowdoc_ref[...] = jnp.concatenate([row_docs] * STACK, 0)

    def masks(self, w, own_block):
        shape = self.rowdoc_ref.shape
        masks = []
        for t in range(self.rows // LANES):
            mask = self.rowdoc_ref[...] == self.doc_ref[w, 0:1, t * LANES : (t + 1) * LANES]
            if own_block:
                row = lax.rem(lax.broadcasted_iota(jnp.int32, shape, 0), self.rows)
                col = lax.broadcasted_iota(jnp.int32, shape, 1) + t * LANES
                mask = mask & (col <= row)
            masks.append(mask)
        return masks

    def scores(self, q, w, own_block):
        s = dot(q, self.k_ref[w], NT)
        return [
            jnp.where(mask, tile(s, t), LOW) for t, mask in enumerate(self.masks(w, own_block))
        ]

    def columns(self, at):
        return [
            pl.ds(pl.multiple_of((at * STACK + i) * self.dim, self.dim), self.dim)
            for i in range(STACK)
        ]

    def stacked_rows(self, at):
        count = STACK * self.rows
        return pl.ds(pl.multiple_of(at * count, count), count)

    def stack(self, ref, at):
        return jnp.concatenate([ref[:, c] for c in self.columns(at)], 0)

    def unstack(self, ref, at, value):
        for i, c in enumerate(self.columns(at)):
            ref[:, c] = value[i * self.rows : (i + 1) * self.rows]


def attend_near(window, q, own_block, m_ref, peak_ref, acc_ref, v_ref, p_ref, refill):
    scale = window.scale * LOG2E

    def attend(w, parts):
        m = m_ref[...]
        p = jnp.concatenate([jnp.exp2(s * scale - m) for s in parts], 1).astype(bf16)
        if p_ref is not None:
            p_ref[w] = p
        acc_ref[...] += dot(p, v_ref[w])

    if own_block:
        parts = window.scores(q, window.last, True)
        top = parts[0]
        for s in parts[1:]:
            top = jnp.maximum(top, s)
        refill(spread(jnp.max(top, axis=1, keepdims=True), top) * scale)
        attend(window.last, parts)
    else:
        refill(None)
    peak_ref[...] = jnp.full_like(peak_ref, LOW)

    def block(w, c):
        parts = window.scores(q, w, False)
        peak = peak_ref[...]
        for s in parts:
            peak = jnp.maximum(peak, s)
        peak_ref[...] = peak
        attend(w, parts)
        return c

    lax.fori_loop(window.lo, window.last, block, 0)
    excess = peak_ref[...] * scale - m_ref[...]

    @pl.when(jnp.max(excess) > HEADROOM)
    def _():
        peak = peak_ref[...]
        refill(jnp.maximum(m_ref[...], spread(jnp.max(peak, axis=1, keepdims=True), peak) * scale))

        def again(w, c):
            attend(w, window.scores(q, w, False))
            return c

        lax.fori_loop(window.lo, window.last, again, 0)
        if own_block:
            attend(window.last, window.scores(q, window.last, True))


def start_kernel(count, heads, *refs):
    refs = list(refs)
    near = [refs.pop(0) for _ in range(count)]
    own, q_ref, acc_out, m_out, l_out = [refs.pop(0) for _ in range(5)]
    k_ref, v_ref, m_ref, peak_ref, acc_ref, doc_ref, rowdoc_ref = refs
    window = Window(near, own, heads, q_ref, k_ref, v_ref, doc_ref, rowdoc_ref)
    dim = window.dim

    def step(at, carry):
        def refill(top):
            m_ref[...] = top
            acc_ref[...] = jnp.zeros_like(acc_ref)

        q = window.stack(q_ref, at)
        attend_near(window, q, True, m_ref, peak_ref, acc_ref, v_ref, None, refill)
        window.unstack(acc_out, at, acc_ref[:, 0:dim])
        m_out[window.stacked_rows(at)] = m_ref[...]
        l_out[window.stacked_rows(at)] = acc_ref[:, dim : 2 * dim]
        return carry

    lax.fori_loop(0, heads // STACK, step, 0)


def far_kernel(count, heads, *refs):
    back = PARTS[0]
    refs = list(refs)
    near = [refs.pop(0) for _ in range(count)]
    own, q_ref, do_ref, acc_in, m_in, l_in = [refs.pop(0) for _ in range(6)]
    out_ref, dq_ref, log_ref, delta_ref = [refs.pop(0) for _ in range(4)]
    dnear = [refs.pop(0) for _ in range(back)]
    k_ref, v_ref, m_ref, peak_ref, acc_ref, doc_ref, rowdoc_ref, p_ref, dqa_ref, dk_ref, dv_ref = (
        refs
    )
    window = Window(near, own, heads, q_ref, k_ref, v_ref, doc_ref, rowdoc_ref)
    dim, tiles = window.dim, window.rows // LANES
    dk_ref[...] = jnp.zeros_like(dk_ref)
    dv_ref[...] = jnp.zeros_like(dv_ref)

    def step(at, carry):
        here = window.stacked_rows(at)

        def refill(top):
            old = m_in[here]
            m_ref[...] = old if top is None else top
            shrink = 1.0 if top is None else jnp.exp2(old - top)
            acc_ref[:, 0:dim] = window.stack(acc_in, at) * shrink
            acc_ref[:, dim : 2 * dim] = l_in[here] * shrink

        q = window.stack(q_ref, at)
        do = window.stack(do_ref, at)
        attend_near(window, q, False, m_ref, peak_ref, acc_ref, v_ref, p_ref, refill)
        total = acc_ref[:, dim : 2 * dim]
        inv = 1.0 / total
        out = (acc_ref[:, 0:dim] * inv).astype(bf16)
        dof = do.astype(f32)
        delta = jnp.sum(dof * out.astype(f32), axis=1, keepdims=True)
        log_ref[here] = m_ref[...] + jnp.log(total) * LOG2E
        delta_ref[here] = spread(delta, total)
        q_inv = (q.astype(f32) * inv).astype(bf16).T
        do_inv = (dof * inv).astype(bf16).T
        dqa_ref[...] = jnp.zeros_like(dqa_ref)

        def grad_block(w, c):
            dp = dot(do, v_ref[w, :, 0:dim], NT)
            delta = delta_ref[here]
            p = p_ref[w]
            parts = [
                (tile(p, t).astype(f32) * (tile(dp, t) - delta)).astype(bf16)
                for t in range(tiles)
            ]
            ds = jnp.concatenate(parts, 1)
            dqa_ref[...] += dot(ds, k_ref[w])
            dk_ref[w] += dot(q_inv, ds)
            dv_ref[w] += dot(do_inv, p)
            return c

        lax.fori_loop(window.lo, back, grad_block, 0)
        window.unstack(out_ref, at, out)
        window.unstack(dq_ref, at, dqa_ref[...] * inv)
        return carry

    lax.fori_loop(0, heads // STACK, step, 0)
    for w in range(back):
        dnear[w][0:dim] = (dk_ref[w] * window.scale).astype(bf16)
        dnear[w][dim : 2 * dim] = dv_ref[w].astype(bf16)


def back_kernel(final, count, heads, *refs):
    refs = list(refs)
    near = [refs.pop(0) for _ in range(count)]
    own, q_ref, do_ref, dq_in, log_ref, delta_ref = [refs.pop(0) for _ in range(6)]
    dq_ref = refs.pop(0)
    dnear = [refs.pop(0) for _ in range(count)]
    down = refs.pop(0) if final else None
    k_ref, v_ref, doc_ref, rowdoc_ref, dqa_ref, dk_ref, dv_ref = refs
    window = Window(near, own, heads, q_ref, k_ref, v_ref, doc_ref, rowdoc_ref)
    dim, scale = window.dim, window.scale
    dk_ref[...] = jnp.zeros_like(dk_ref)
    dv_ref[...] = jnp.zeros_like(dv_ref)

    def step(at, carry):
        here = window.stacked_rows(at)
        q = window.stack(q_ref, at)
        do = window.stack(do_ref, at)
        q_t = q.T
        do_t = do.T
        dqa_ref[...] = window.stack(dq_in, at)

        def grad_block(w, own_block):
            s = dot(q, k_ref[w], NT)
            dp = dot(do, v_ref[w], NT)
            top = log_ref[here]
            delta = delta_ref[here]
            probs = []
            dscores = []
            for t, mask in enumerate(window.masks(w, own_block)):
                p = jnp.where(mask, jnp.exp2(tile(s, t) * (scale * LOG2E) - top), 0.0)
                probs.append(p.astype(bf16))
                dscores.append((p * (tile(dp, t) - delta)).astype(bf16))
            ds = jnp.concatenate(dscores, 1)
            dqa_ref[...] += dot(ds, k_ref[w])
            dk_ref[w] += dot(q_t, ds)
            dv_ref[w] += dot(do_t, jnp.concatenate(probs, 1))

        def near_block(w, c):
            grad_block(w, False)
            return c

        lax.fori_loop(window.lo, window.last, near_block, 0)
        if final:
            grad_block(window.last, True)
            window.unstack(dq_ref, at, (dqa_ref[...] * scale).astype(bf16))
        else:
            window.unstack(dq_ref, at, dqa_ref[...])
        return carry

    lax.fori_loop(0, heads // STACK, step, 0)
    for w in range(count):
        dnear[w][0:dim] = (dk_ref[w] * scale).astype(bf16)
        dnear[w][dim : 2 * dim] = dv_ref[w].astype(bf16)
    if final:
        down[0:dim] = dk_ref[count] * scale
        down[dim : 2 * dim] = dv_ref[count]


def sum_kernel(down, *refs):
    *terms, dk_ref, dv_ref = refs
    total = down[...]
    for term in terms:
        total = total + term[...].astype(f32)
    dim = dk_ref.shape[1]
    dk_ref[...] = total[0:dim].T.astype(bf16)
    dv_ref[...] = total[dim : 2 * dim].T.astype(bf16)


def call(kernel, near, args, outs, scratch, heads, name, plain=0):
    args = [*near, *args]
    held = [pltpu.with_memory_space_constraint(a, pltpu.VMEM) for a in args[: len(args) - plain]]
    args = held + args[len(held) :]
    vmem = pl.BlockSpec(memory_space=pltpu.VMEM)
    return pl.pallas_call(
        lambda *refs: kernel(len(near), heads, *refs),
        out_shape=outs,
        in_specs=[vmem] * len(args),
        out_specs=[vmem] * len(outs),
        scratch_shapes=scratch,
        compiler_params=pltpu.CompilerParams(vmem_limit_bytes=VMEM_BYTES),
        name=name,
    )(*args)


def attention_start(near, own, queries, dim):
    rows, width = queries.shape
    heads, blocks, stacked = width // dim, len(near) + 1, STACK * rows
    by_head = pltpu.VMEM((heads * rows, LANES), f32)
    outs = [pltpu.VMEM((rows, width), f32), by_head, by_head]
    scratch = [
        pltpu.VMEM((blocks, rows, dim), bf16),
        pltpu.VMEM((blocks, rows, 2 * dim), bf16),
        pltpu.VMEM((stacked, LANES), f32),
        pltpu.VMEM((stacked, LANES), f32),
        pltpu.VMEM((stacked, 2 * dim), f32),
        pltpu.VMEM((blocks, 8, rows), f32),
        pltpu.VMEM((stacked, LANES), f32),
    ]
    args = (own, queries)
    return call(start_kernel, near, args, outs, scratch, heads, "forward_near", plain=1)


def attention_far(near, own, queries, grad_out, state, dim):
    rows, width = queries.shape
    heads, blocks, stacked = width // dim, len(near), STACK * rows
    by_head = pltpu.VMEM((heads * rows, LANES), f32)
    outs = [jax.ShapeDtypeStruct((rows, width), bf16), pltpu.VMEM((rows, width), f32)]
    outs += [by_head, by_head] + [pltpu.VMEM((2 * dim, rows), bf16)] * PARTS[0]
    scratch = [
        pltpu.VMEM((blocks, rows, dim), bf16),
        pltpu.VMEM((blocks, rows, 2 * dim), bf16),
        pltpu.VMEM((stacked, LANES), f32),
        pltpu.VMEM((stacked, LANES), f32),
        pltpu.VMEM((stacked, 2 * dim), f32),
        pltpu.VMEM((blocks + 1, 8, rows), f32),
        pltpu.VMEM((stacked, LANES), f32),
        pltpu.VMEM((blocks, stacked, rows), bf16),
        pltpu.VMEM((stacked, dim), f32),
        pltpu.VMEM((PARTS[0], dim, rows), f32),
        pltpu.VMEM((PARTS[0], dim, rows), f32),
    ]
    args = (own, queries, grad_out, *state)
    return call(far_kernel, near, args, outs, scratch, heads, "attention_far")


def attention_back(final, near, own, queries, grad_out, dq, log_total, delta, dim):
    rows, width = queries.shape
    heads, blocks, stacked = width // dim, len(near) + int(final), STACK * rows
    if final:
        outs = [jax.ShapeDtypeStruct((rows, width), bf16)]
    else:
        outs = [pltpu.VMEM((rows, width), f32)]
    outs += [pltpu.VMEM((2 * dim, rows), bf16)] * len(near)
    if final:
        outs += [pltpu.VMEM((2 * dim, rows), f32)]
    scratch = [
        pltpu.VMEM((blocks, rows, dim), bf16),
        pltpu.VMEM((blocks, rows, dim), bf16),
        pltpu.VMEM((len(near) + 1, 8, rows), f32),
        pltpu.VMEM((stacked, LANES), f32),
        pltpu.VMEM((stacked, dim), f32),
        pltpu.VMEM((blocks, dim, rows), f32),
        pltpu.VMEM((blocks, dim, rows), f32),
    ]
    args = (own, queries, grad_out, dq, log_total, delta)
    name = "backward_final" if final else "backward_mid"
    return call(partial(back_kernel, final), near, args, outs, scratch, heads, name)


def sum_terms(down, terms, dim):
    rows = down.shape[1]
    out = jax.ShapeDtypeStruct((rows, dim), bf16)
    return call(
        lambda count, heads, *refs: sum_kernel(*refs), [down], terms, [out, out], [], 1, "sum_terms"
    )


def shift(block, by):
    axes = ("outer", "inner")
    count = lax.axis_size(axes)
    return lax.ppermute(block, axes, [(i, (i + by) % count) for i in range(count)])


def on_device(queries, keys, values, grad_out, doc_ids):
    rows, dim = keys.shape
    reach = lax.axis_size("inner")
    docs = doc_ids.astype(bf16).reshape(rows // (2 * dim), 2 * dim)
    docs = jnp.pad(docs, ((0, DOC_ROWS - docs.shape[0]), (0, 0)))
    own = jnp.concatenate([jnp.concatenate([keys, values], 1), docs], 0)
    behind = [shift(own, reach - i) for i in range(reach)]
    state = attention_start(behind[FAR:], own, queries, dim)
    attn_out, dq, log_total, delta, *grads = attention_far(
        behind[:FAR], own, queries, grad_out, state, dim
    )
    terms = [shift(g, i - reach) for i, g in enumerate(grads)]
    done = PARTS[0]
    for part in PARTS[1:]:
        final = done == reach
        dq, *grads = attention_back(
            final, behind[done : done + part], own, queries, grad_out, dq, log_total, delta, dim
        )
        if not final:
            terms, grads = lax.optimization_barrier((terms, grads))
            terms += [shift(g, done + i - reach) for i, g in enumerate(grads)]
        done += part
    grad_k, grad_v = sum_terms(grads[-1], terms, dim)
    return (attn_out, dq, grad_k, grad_v)


def solution(mesh):
    rows = P(("outer", "inner"), None)
    return jax.shard_map(
        on_device,
        mesh=mesh,
        in_specs=(rows, rows, rows, rows, P(("outer", "inner"))),
        out_specs=(rows, rows, rows, rows),
        check_vma=False,
    )
```

```python
from functools import partial

import jax
import jax.numpy as jnp
from jax import lax
from jax.experimental import pallas as pl
from jax.experimental.pallas import tpu as pltpu
from jax.sharding import PartitionSpec as P

LOG2E = 1.4426950408889634
LOW = -1e30
HEADROOM = 64.0
LANES = 128
DOC_ROWS = 16
STACK = 4
VMEM_BYTES = 34 * 1024 * 1024
f32 = jnp.float32
bf16 = jnp.bfloat16
NN = (((1,), (0,)), ((), ()))
NT = (((1,), (1,)), ((), ()))


def dot(a, b, dims=NN):
    return lax.dot_general(a, b, dims, preferred_element_type=f32)


def tile(x, t):
    return x[:, t * LANES : (t + 1) * LANES]


def spread(column, like):
    return jnp.broadcast_to(column, like.shape)


class Window:
    def __init__(self, near, own, heads, q_ref, k_ref, v_ref, doc_ref, rowdoc_ref):
        rows, width = q_ref.shape
        self.rows, self.dim = rows, width // heads
        self.last = len(near)
        self.scale = self.dim ** (-0.5)
        self.k_ref, self.doc_ref, self.rowdoc_ref = k_ref, doc_ref, rowdoc_ref
        for w, ref in enumerate(near + [own]):
            if w < k_ref.shape[0]:
                k_ref[w] = ref[0:rows, 0 : self.dim]
                v_ref[w, :, 0 : self.dim] = ref[0:rows, self.dim : 2 * self.dim]
                if v_ref.shape[2] > self.dim:
                    v_ref[w, :, self.dim : 2 * self.dim] = jnp.ones((rows, self.dim), bf16)
            docs = ref[rows : rows + DOC_ROWS, :].astype(f32)
            for t in range(rows // LANES):
                part = docs[t // 2 : t // 2 + 1, (t % 2) * LANES : (t % 2 + 1) * LANES]
                doc_ref[w, 0:1, t * LANES : (t + 1) * LANES] = part
        first = jnp.broadcast_to(doc_ref[self.last, 0:1, 0:1], (1, LANES))
        spare = jnp.zeros((1, LANES), f32)
        for w in range(self.last):
            end = jnp.broadcast_to(doc_ref[w, 0:1, rows - 1 : rows], (1, LANES))
            spare = spare + jnp.where(end == first, 0.0, 1.0)
        self.lo = jnp.max(spare).astype(jnp.int32)
        row_docs = jnp.broadcast_to(doc_ref[self.last, 0:1, :], (LANES, rows)).T
        rowdoc_ref[...] = jnp.concatenate([row_docs] * STACK, 0)

    def masks(self, w, own_block):
        shape = self.rowdoc_ref.shape
        masks = []
        for t in range(self.rows // LANES):
            mask = self.rowdoc_ref[...] == self.doc_ref[w, 0:1, t * LANES : (t + 1) * LANES]
            if own_block:
                row = lax.rem(lax.broadcasted_iota(jnp.int32, shape, 0), self.rows)
                col = lax.broadcasted_iota(jnp.int32, shape, 1) + t * LANES
                mask = mask & (col <= row)
            masks.append(mask)
        return masks

    def scores(self, q, w, own_block):
        s = dot(q, self.k_ref[w], NT)
        return [
            jnp.where(mask, tile(s, t), LOW) for t, mask in enumerate(self.masks(w, own_block))
        ]

    def columns(self, at):
        return [
            pl.ds(pl.multiple_of((at * STACK + i) * self.dim, self.dim), self.dim)
            for i in range(STACK)
        ]

    def stacked_rows(self, at):
        count = STACK * self.rows
        return pl.ds(pl.multiple_of(at * count, count), count)

    def stack(self, ref, at):
        return jnp.concatenate([ref[:, c] for c in self.columns(at)], 0)

    def unstack(self, ref, at, value):
        for i, c in enumerate(self.columns(at)):
            ref[:, c] = value[i * self.rows : (i + 1) * self.rows]


def attend_near(window, q, own_block, m_ref, peak_ref, acc_ref, v_ref, p_ref, refill):
    scale = window.scale * LOG2E

    def attend(w, parts):
        m = m_ref[...]
        p = jnp.concatenate([jnp.exp2(s * scale - m) for s in parts], 1).astype(bf16)
        if p_ref is not None:
            p_ref[w] = p
        acc_ref[...] += dot(p, v_ref[w])

    if own_block:
        parts = window.scores(q, window.last, True)
        top = parts[0]
        for s in parts[1:]:
            top = jnp.maximum(top, s)
        refill(spread(jnp.max(top, axis=1, keepdims=True), top) * scale)
        attend(window.last, parts)
    else:
        refill(None)
    peak_ref[...] = jnp.full_like(peak_ref, LOW)

    def block(w, c):
        parts = window.scores(q, w, False)
        peak = peak_ref[...]
        for s in parts:
            peak = jnp.maximum(peak, s)
        peak_ref[...] = peak
        attend(w, parts)
        return c

    lax.fori_loop(window.lo, window.last, block, 0)
    excess = peak_ref[...] * scale - m_ref[...]

    @pl.when(jnp.max(excess) > HEADROOM)
    def _():
        peak = peak_ref[...]
        refill(jnp.maximum(m_ref[...], spread(jnp.max(peak, axis=1, keepdims=True), peak) * scale))

        def again(w, c):
            attend(w, window.scores(q, w, False))
            return c

        lax.fori_loop(window.lo, window.last, again, 0)
        if own_block:
            attend(window.last, window.scores(q, window.last, True))


def start_kernel(count, heads, *refs):
    refs = list(refs)
    near = [refs.pop(0) for _ in range(count)]
    own, q_ref, acc_out, m_out, l_out = [refs.pop(0) for _ in range(5)]
    k_ref, v_ref, m_ref, peak_ref, acc_ref, doc_ref, rowdoc_ref = refs
    window = Window(near, own, heads, q_ref, k_ref, v_ref, doc_ref, rowdoc_ref)
    dim = window.dim

    def step(at, carry):
        def refill(top):
            m_ref[...] = top
            acc_ref[...] = jnp.zeros_like(acc_ref)

        q = window.stack(q_ref, at)
        attend_near(window, q, True, m_ref, peak_ref, acc_ref, v_ref, None, refill)
        window.unstack(acc_out, at, acc_ref[:, 0:dim])
        m_out[window.stacked_rows(at)] = m_ref[...]
        l_out[window.stacked_rows(at)] = acc_ref[:, dim : 2 * dim]
        return carry

    lax.fori_loop(0, heads // STACK, step, 0)


def pieces(ref, count):
    rows = ref.shape[0] // count
    return [ref.at[pl.ds(i * rows, rows)] for i in range(count)]


def far_kernel(half, heads, *refs):
    refs = list(refs)
    back = half + 1
    near = [refs.pop(0), *pieces(refs.pop(0), half)]
    own, q_ref, do_ref, acc_in, m_in, l_in = [refs.pop(0) for _ in range(6)]
    out_ref, dq_ref, log_ref, delta_ref = [refs.pop(0) for _ in range(4)]
    dnear = [refs.pop(0), *pieces(refs.pop(0), half)]
    k_ref, v_ref, m_ref, peak_ref, acc_ref, doc_ref, rowdoc_ref, p_ref, dqa_ref, dk_ref, dv_ref = (
        refs
    )
    window = Window(near, own, heads, q_ref, k_ref, v_ref, doc_ref, rowdoc_ref)
    dim, tiles = window.dim, window.rows // LANES
    dk_ref[...] = jnp.zeros_like(dk_ref)
    dv_ref[...] = jnp.zeros_like(dv_ref)

    def step(at, carry):
        here = window.stacked_rows(at)

        def refill(top):
            old = m_in[here]
            m_ref[...] = old if top is None else top
            shrink = 1.0 if top is None else jnp.exp2(old - top)
            acc_ref[:, 0:dim] = window.stack(acc_in, at) * shrink
            acc_ref[:, dim : 2 * dim] = l_in[here] * shrink

        q = window.stack(q_ref, at)
        do = window.stack(do_ref, at)
        attend_near(window, q, False, m_ref, peak_ref, acc_ref, v_ref, p_ref, refill)
        total = acc_ref[:, dim : 2 * dim]
        inv = 1.0 / total
        out = (acc_ref[:, 0:dim] * inv).astype(bf16)
        dof = do.astype(f32)
        delta = jnp.sum(dof * out.astype(f32), axis=1, keepdims=True)
        log_ref[here] = m_ref[...] + jnp.log(total) * LOG2E
        delta_ref[here] = spread(delta, total)
        q_inv = (q.astype(f32) * inv).astype(bf16).T
        do_inv = (dof * inv).astype(bf16).T
        dqa_ref[...] = jnp.zeros_like(dqa_ref)

        def grad_block(w, c):
            dp = dot(do, v_ref[w, :, 0:dim], NT)
            delta = delta_ref[here]
            p = p_ref[w]
            parts = [
                (tile(p, t).astype(f32) * (tile(dp, t) - delta)).astype(bf16)
                for t in range(tiles)
            ]
            ds = jnp.concatenate(parts, 1)
            dqa_ref[...] += dot(ds, k_ref[w])
            dk_ref[w] += dot(q_inv, ds)
            dv_ref[w] += dot(do_inv, p)
            return c

        lax.fori_loop(window.lo, back, grad_block, 0)
        window.unstack(out_ref, at, out)
        window.unstack(dq_ref, at, dqa_ref[...] * inv)
        return carry

    lax.fori_loop(0, heads // STACK, step, 0)
    for w in range(back):
        dnear[w][0:dim] = (dk_ref[w] * window.scale).astype(bf16)
        dnear[w][dim : 2 * dim] = dv_ref[w].astype(bf16)


def back_kernel(final, count, heads, *refs):
    refs = list(refs)
    near = [refs.pop(0) for _ in range(count)]
    own, q_ref, do_ref, dq_in, log_ref, delta_ref = [refs.pop(0) for _ in range(6)]
    dq_ref = refs.pop(0)
    dnear = [refs.pop(0) for _ in range(count)]
    down = refs.pop(0) if final else None
    k_ref, v_ref, doc_ref, rowdoc_ref, dqa_ref, dk_ref, dv_ref = refs
    window = Window(near, own, heads, q_ref, k_ref, v_ref, doc_ref, rowdoc_ref)
    dim, scale = window.dim, window.scale
    dk_ref[...] = jnp.zeros_like(dk_ref)
    dv_ref[...] = jnp.zeros_like(dv_ref)

    def step(at, carry):
        here = window.stacked_rows(at)
        q = window.stack(q_ref, at)
        do = window.stack(do_ref, at)
        q_t = q.T
        do_t = do.T
        dqa_ref[...] = window.stack(dq_in, at)

        def grad_block(w, own_block):
            s = dot(q, k_ref[w], NT)
            dp = dot(do, v_ref[w], NT)
            top = log_ref[here]
            delta = delta_ref[here]
            probs = []
            dscores = []
            for t, mask in enumerate(window.masks(w, own_block)):
                p = jnp.where(mask, jnp.exp2(tile(s, t) * (scale * LOG2E) - top), 0.0)
                probs.append(p.astype(bf16))
                dscores.append((p * (tile(dp, t) - delta)).astype(bf16))
            ds = jnp.concatenate(dscores, 1)
            dqa_ref[...] += dot(ds, k_ref[w])
            dk_ref[w] += dot(q_t, ds)
            dv_ref[w] += dot(do_t, jnp.concatenate(probs, 1))

        def near_block(w, c):
            grad_block(w, False)
            return c

        lax.fori_loop(window.lo, window.last, near_block, 0)
        if final:
            grad_block(window.last, True)
            window.unstack(dq_ref, at, (dqa_ref[...] * scale).astype(bf16))
        else:
            window.unstack(dq_ref, at, dqa_ref[...])
        return carry

    lax.fori_loop(0, heads // STACK, step, 0)
    for w in range(count):
        dnear[w][0:dim] = (dk_ref[w] * scale).astype(bf16)
        dnear[w][dim : 2 * dim] = dv_ref[w].astype(bf16)
    if final:
        down[0:dim] = dk_ref[count] * scale
        down[dim : 2 * dim] = dv_ref[count]


def sum_kernel(half, down, older, *refs):
    *terms, dk_ref, dv_ref = refs
    total = down[...] + pieces(older, half)[-1][...].astype(f32)
    for term in terms:
        total = total + term[...].astype(f32)
    dim = dk_ref.shape[1]
    dk_ref[...] = total[0:dim].T.astype(bf16)
    dv_ref[...] = total[dim : 2 * dim].T.astype(bf16)


def call(kernel, near, args, outs, scratch, heads, name, plain=0):
    args = [*near, *args]
    held = [pltpu.with_memory_space_constraint(a, pltpu.VMEM) for a in args[: len(args) - plain]]
    args = held + args[len(held) :]
    vmem = pl.BlockSpec(memory_space=pltpu.VMEM)
    return pl.pallas_call(
        lambda *refs: kernel(len(near), heads, *refs),
        out_shape=outs,
        in_specs=[vmem] * len(args),
        out_specs=[vmem] * len(outs),
        scratch_shapes=scratch,
        compiler_params=pltpu.CompilerParams(vmem_limit_bytes=VMEM_BYTES),
        name=name,
    )(*args)


def attention_start(near, own, queries, dim):
    rows, width = queries.shape
    heads, blocks, stacked = width // dim, len(near) + 1, STACK * rows
    by_head = pltpu.VMEM((heads * rows, LANES), f32)
    outs = [pltpu.VMEM((rows, width), f32), by_head, by_head]
    scratch = [
        pltpu.VMEM((blocks, rows, dim), bf16),
        pltpu.VMEM((blocks, rows, 2 * dim), bf16),
        pltpu.VMEM((stacked, LANES), f32),
        pltpu.VMEM((stacked, LANES), f32),
        pltpu.VMEM((stacked, 2 * dim), f32),
        pltpu.VMEM((blocks, 8, rows), f32),
        pltpu.VMEM((stacked, LANES), f32),
    ]
    args = (own, queries)
    return call(start_kernel, near, args, outs, scratch, heads, "forward_near", plain=1)


def attention_far(oldest, older, half, own, queries, grad_out, state, dim):
    rows, width = queries.shape
    heads, blocks, stacked = width // dim, half + 1, STACK * rows
    by_head = pltpu.VMEM((heads * rows, LANES), f32)
    outs = [jax.ShapeDtypeStruct((rows, width), bf16), pltpu.VMEM((rows, width), f32)]
    outs += [by_head, by_head, pltpu.VMEM((2 * dim, rows), bf16)]
    outs += [pltpu.VMEM((half * 2 * dim, rows), bf16)]
    scratch = [
        pltpu.VMEM((blocks, rows, dim), bf16),
        pltpu.VMEM((blocks, rows, 2 * dim), bf16),
        pltpu.VMEM((stacked, LANES), f32),
        pltpu.VMEM((stacked, LANES), f32),
        pltpu.VMEM((stacked, 2 * dim), f32),
        pltpu.VMEM((blocks + 1, 8, rows), f32),
        pltpu.VMEM((stacked, LANES), f32),
        pltpu.VMEM((blocks, stacked, rows), bf16),
        pltpu.VMEM((stacked, dim), f32),
        pltpu.VMEM((blocks, dim, rows), f32),
        pltpu.VMEM((blocks, dim, rows), f32),
    ]
    args = (own, queries, grad_out, *state)
    kernel = lambda count, heads, *refs: far_kernel(half, heads, *refs)
    return call(kernel, [oldest, older], args, outs, scratch, heads, "attention_far")


def attention_back(final, near, own, queries, grad_out, dq, log_total, delta, dim):
    rows, width = queries.shape
    heads, blocks, stacked = width // dim, len(near) + int(final), STACK * rows
    if final:
        outs = [jax.ShapeDtypeStruct((rows, width), bf16)]
    else:
        outs = [pltpu.VMEM((rows, width), f32)]
    outs += [pltpu.VMEM((2 * dim, rows), bf16)] * len(near)
    if final:
        outs += [pltpu.VMEM((2 * dim, rows), f32)]
    scratch = [
        pltpu.VMEM((blocks, rows, dim), bf16),
        pltpu.VMEM((blocks, rows, dim), bf16),
        pltpu.VMEM((len(near) + 1, 8, rows), f32),
        pltpu.VMEM((stacked, LANES), f32),
        pltpu.VMEM((stacked, dim), f32),
        pltpu.VMEM((blocks, dim, rows), f32),
        pltpu.VMEM((blocks, dim, rows), f32),
    ]
    args = (own, queries, grad_out, dq, log_total, delta)
    name = "backward_final" if final else "backward_mid"
    return call(partial(back_kernel, final), near, args, outs, scratch, heads, name)


def join_kernel(count, heads, *refs):
    *blocks, out = refs
    for piece, block in zip(pieces(out, len(blocks)), blocks):
        piece[...] = block[...]


def join(blocks):
    rows, width = blocks[0].shape
    outs = [pltpu.VMEM((len(blocks) * rows, width), bf16)]
    return call(join_kernel, [], blocks, outs, [], 1, "join")[0]


def sum_terms(down, older, half, terms, dim):
    rows = down.shape[1]
    out = jax.ShapeDtypeStruct((rows, dim), bf16)
    kernel = lambda count, heads, *refs: sum_kernel(half, *refs)
    return call(kernel, [down, older], terms, [out, out], [], 1, "sum_terms")


def shift(block, by):
    axes = ("outer", "inner")
    count = lax.axis_size(axes)
    return lax.ppermute(block, axes, [(i, (i + by) % count) for i in range(count)])


def on_device(queries, keys, values, grad_out, doc_ids):
    rows, dim = keys.shape
    reach = lax.axis_size("inner")
    docs = doc_ids.astype(bf16).reshape(rows // (2 * dim), 2 * dim)
    docs = jnp.pad(docs, ((0, DOC_ROWS - docs.shape[0]), (0, 0)))
    own = jnp.concatenate([jnp.concatenate([keys, values], 1), docs], 0)
    half = reach // 2
    near = [shift(own, by) for by in range(half - 1, 0, -1)]
    oldest = shift(own, reach)
    near, oldest = lax.optimization_barrier((near, oldest))
    older = shift(join([*near, own]), half)
    state = attention_start(near, own, queries, dim)
    attn_out, dq, log_total, delta, oldest_grads, older_grads = attention_far(
        oldest, older, half, own, queries, grad_out, state, dim
    )
    oldest_terms = shift(oldest_grads, -reach)
    older_terms = shift(older_grads, -half)
    dq, *grads = attention_back(
        False, near, own, queries, grad_out, dq, log_total, delta, dim
    )
    size = 2 * dim
    terms = [oldest_terms]
    for i, g in enumerate(grads):
        came = older_terms[i * size : (i + 1) * size]
        g = (g.astype(f32) + came.astype(f32)).astype(bf16)
        terms.append(shift(g, i + 1 - half))
    grad_q, own_grads = attention_back(
        True, [], own, queries, grad_out, dq, log_total, delta, dim
    )
    grad_k, grad_v = sum_terms(own_grads, older_terms, half, terms, dim)
    return (attn_out, grad_q, grad_k, grad_v)


def solution(mesh):
    rows = P(("outer", "inner"), None)
    return jax.shard_map(
        on_device,
        mesh=mesh,
        in_specs=(rows, rows, rows, rows, P(("outer", "inner"))),
        out_specs=(rows, rows, rows, rows),
        check_vma=False,
    )
```

```python
from functools import partial

import jax
import jax.numpy as jnp
from jax import lax
from jax.experimental import pallas as pl
from jax.experimental.pallas import tpu as pltpu
from jax.sharding import PartitionSpec as P

LOG2E = 1.4426950408889634
LOW = -1e30
HEADROOM = 64.0
LANES = 128
DOC_ROWS = 16
STACK = 4
VMEM_BYTES = 34 * 1024 * 1024
f32 = jnp.float32
bf16 = jnp.bfloat16
NN = (((1,), (0,)), ((), ()))
NT = (((1,), (1,)), ((), ()))


def dot(a, b, dims=NN):
    return lax.dot_general(a, b, dims, preferred_element_type=f32)


def tile(x, t):
    return x[:, t * LANES : (t + 1) * LANES]


def spread(column, like):
    return jnp.broadcast_to(column, like.shape)


class Window:
    def __init__(self, near, own, heads, q_ref, k_ref, v_ref, doc_ref, rowdoc_ref):
        rows, width = q_ref.shape
        self.rows, self.dim = rows, width // heads
        self.last = len(near)
        self.scale = self.dim ** (-0.5)
        self.k_ref, self.doc_ref, self.rowdoc_ref = k_ref, doc_ref, rowdoc_ref
        for w, ref in enumerate(near + [own]):
            if w < k_ref.shape[0]:
                k_ref[w] = ref[0:rows, 0 : self.dim]
                v_ref[w, :, 0 : self.dim] = ref[0:rows, self.dim : 2 * self.dim]
                if v_ref.shape[2] > self.dim:
                    v_ref[w, :, self.dim : 2 * self.dim] = jnp.ones((rows, self.dim), bf16)
            docs = ref[rows : rows + DOC_ROWS, :].astype(f32)
            for t in range(rows // LANES):
                part = docs[t // 2 : t // 2 + 1, (t % 2) * LANES : (t % 2 + 1) * LANES]
                doc_ref[w, 0:1, t * LANES : (t + 1) * LANES] = part
        first = jnp.broadcast_to(doc_ref[self.last, 0:1, 0:1], (1, LANES))
        spare = jnp.zeros((1, LANES), f32)
        for w in range(self.last):
            end = jnp.broadcast_to(doc_ref[w, 0:1, rows - 1 : rows], (1, LANES))
            spare = spare + jnp.where(end == first, 0.0, 1.0)
        self.lo = jnp.max(spare).astype(jnp.int32)
        row_docs = jnp.broadcast_to(doc_ref[self.last, 0:1, :], (LANES, rows)).T
        rowdoc_ref[...] = jnp.concatenate([row_docs] * STACK, 0)

    def masks(self, w, own_block):
        shape = self.rowdoc_ref.shape
        masks = []
        for t in range(self.rows // LANES):
            mask = self.rowdoc_ref[...] == self.doc_ref[w, 0:1, t * LANES : (t + 1) * LANES]
            if own_block:
                row = lax.rem(lax.broadcasted_iota(jnp.int32, shape, 0), self.rows)
                col = lax.broadcasted_iota(jnp.int32, shape, 1) + t * LANES
                mask = mask & (col <= row)
            masks.append(mask)
        return masks

    def scores(self, q, w, own_block):
        s = dot(q, self.k_ref[w], NT)
        return [
            jnp.where(mask, tile(s, t), LOW) for t, mask in enumerate(self.masks(w, own_block))
        ]

    def columns(self, at):
        return [
            pl.ds(pl.multiple_of((at * STACK + i) * self.dim, self.dim), self.dim)
            for i in range(STACK)
        ]

    def stacked_rows(self, at):
        count = STACK * self.rows
        return pl.ds(pl.multiple_of(at * count, count), count)

    def stack(self, ref, at):
        return jnp.concatenate([ref[:, c] for c in self.columns(at)], 0)

    def unstack(self, ref, at, value):
        for i, c in enumerate(self.columns(at)):
            ref[:, c] = value[i * self.rows : (i + 1) * self.rows]


def attend_near(window, q, own_block, m_ref, peak_ref, acc_ref, v_ref, p_ref, refill):
    scale = window.scale * LOG2E

    def attend(w, parts):
        m = m_ref[...]
        p = jnp.concatenate([jnp.exp2(s * scale - m) for s in parts], 1).astype(bf16)
        if p_ref is not None:
            p_ref[w] = p
        acc_ref[...] += dot(p, v_ref[w])

    if own_block:
        parts = window.scores(q, window.last, True)
        top = parts[0]
        for s in parts[1:]:
            top = jnp.maximum(top, s)
        refill(spread(jnp.max(top, axis=1, keepdims=True), top) * scale)
        attend(window.last, parts)
    else:
        refill(None)
    peak_ref[...] = jnp.full_like(peak_ref, LOW)

    def block(w, c):
        parts = window.scores(q, w, False)
        peak = peak_ref[...]
        for s in parts:
            peak = jnp.maximum(peak, s)
        peak_ref[...] = peak
        attend(w, parts)
        return c

    lax.fori_loop(window.lo, window.last, block, 0)
    excess = peak_ref[...] * scale - m_ref[...]

    @pl.when(jnp.max(excess) > HEADROOM)
    def _():
        peak = peak_ref[...]
        refill(jnp.maximum(m_ref[...], spread(jnp.max(peak, axis=1, keepdims=True), peak) * scale))

        def again(w, c):
            attend(w, window.scores(q, w, False))
            return c

        lax.fori_loop(window.lo, window.last, again, 0)
        if own_block:
            attend(window.last, window.scores(q, window.last, True))


def start_kernel(count, heads, *refs):
    refs = list(refs)
    near = [refs.pop(0) for _ in range(count)]
    own, q_ref, acc_out, m_out, l_out = [refs.pop(0) for _ in range(5)]
    k_ref, v_ref, m_ref, peak_ref, acc_ref, doc_ref, rowdoc_ref = refs
    window = Window(near, own, heads, q_ref, k_ref, v_ref, doc_ref, rowdoc_ref)
    dim = window.dim

    def step(at, carry):
        def refill(top):
            m_ref[...] = top
            acc_ref[...] = jnp.zeros_like(acc_ref)

        q = window.stack(q_ref, at)
        attend_near(window, q, True, m_ref, peak_ref, acc_ref, v_ref, None, refill)
        window.unstack(acc_out, at, acc_ref[:, 0:dim])
        m_out[window.stacked_rows(at)] = m_ref[...]
        l_out[window.stacked_rows(at)] = acc_ref[:, dim : 2 * dim]
        return carry

    lax.fori_loop(0, heads // STACK, step, 0)


def pieces(ref, count):
    rows = ref.shape[0] // count
    return [ref.at[pl.ds(i * rows, rows)] for i in range(count)]


def far_kernel(half, heads, *refs):
    refs = list(refs)
    back = half + 1
    near = [refs.pop(0) for _ in range(back)]
    own, q_ref, do_ref, acc_in, m_in, l_in = [refs.pop(0) for _ in range(6)]
    out_ref, dq_ref, log_ref, delta_ref = [refs.pop(0) for _ in range(4)]
    dnear = [refs.pop(0), *pieces(refs.pop(0), half)]
    k_ref, v_ref, m_ref, peak_ref, acc_ref, doc_ref, rowdoc_ref, p_ref, dqa_ref, dk_ref, dv_ref = (
        refs
    )
    window = Window(near, own, heads, q_ref, k_ref, v_ref, doc_ref, rowdoc_ref)
    dim, tiles = window.dim, window.rows // LANES
    dk_ref[...] = jnp.zeros_like(dk_ref)
    dv_ref[...] = jnp.zeros_like(dv_ref)

    def step(at, carry):
        here = window.stacked_rows(at)

        def refill(top):
            old = m_in[here]
            m_ref[...] = old if top is None else top
            shrink = 1.0 if top is None else jnp.exp2(old - top)
            acc_ref[:, 0:dim] = window.stack(acc_in, at) * shrink
            acc_ref[:, dim : 2 * dim] = l_in[here] * shrink

        q = window.stack(q_ref, at)
        do = window.stack(do_ref, at)
        attend_near(window, q, False, m_ref, peak_ref, acc_ref, v_ref, p_ref, refill)
        total = acc_ref[:, dim : 2 * dim]
        inv = 1.0 / total
        out = (acc_ref[:, 0:dim] * inv).astype(bf16)
        dof = do.astype(f32)
        delta = jnp.sum(dof * out.astype(f32), axis=1, keepdims=True)
        log_ref[here] = m_ref[...] + jnp.log(total) * LOG2E
        delta_ref[here] = spread(delta, total)
        q_inv = (q.astype(f32) * inv).astype(bf16).T
        do_inv = (dof * inv).astype(bf16).T
        dqa_ref[...] = jnp.zeros_like(dqa_ref)

        def grad_block(w, c):
            dp = dot(do, v_ref[w, :, 0:dim], NT)
            delta = delta_ref[here]
            p = p_ref[w]
            parts = [
                (tile(p, t).astype(f32) * (tile(dp, t) - delta)).astype(bf16)
                for t in range(tiles)
            ]
            ds = jnp.concatenate(parts, 1)
            dqa_ref[...] += dot(ds, k_ref[w])
            dk_ref[w] += dot(q_inv, ds)
            dv_ref[w] += dot(do_inv, p)
            return c

        lax.fori_loop(window.lo, back, grad_block, 0)
        window.unstack(out_ref, at, out)
        window.unstack(dq_ref, at, dqa_ref[...] * inv)
        return carry

    lax.fori_loop(0, heads // STACK, step, 0)
    for w in range(back):
        dnear[w][0:dim] = (dk_ref[w] * window.scale).astype(bf16)
        dnear[w][dim : 2 * dim] = dv_ref[w].astype(bf16)


def back_kernel(final, count, heads, *refs):
    refs = list(refs)
    near = [refs.pop(0) for _ in range(count)]
    own, q_ref, do_ref, dq_in, log_ref, delta_ref = [refs.pop(0) for _ in range(6)]
    dq_ref = refs.pop(0)
    dnear = [refs.pop(0) for _ in range(count)]
    down = refs.pop(0) if final else None
    k_ref, v_ref, doc_ref, rowdoc_ref, dqa_ref, dk_ref, dv_ref = refs
    window = Window(near, own, heads, q_ref, k_ref, v_ref, doc_ref, rowdoc_ref)
    dim, scale = window.dim, window.scale
    dk_ref[...] = jnp.zeros_like(dk_ref)
    dv_ref[...] = jnp.zeros_like(dv_ref)

    def step(at, carry):
        here = window.stacked_rows(at)
        q = window.stack(q_ref, at)
        do = window.stack(do_ref, at)
        q_t = q.T
        do_t = do.T
        dqa_ref[...] = window.stack(dq_in, at)

        def grad_block(w, own_block):
            s = dot(q, k_ref[w], NT)
            dp = dot(do, v_ref[w], NT)
            top = log_ref[here]
            delta = delta_ref[here]
            probs = []
            dscores = []
            for t, mask in enumerate(window.masks(w, own_block)):
                p = jnp.where(mask, jnp.exp2(tile(s, t) * (scale * LOG2E) - top), 0.0)
                probs.append(p.astype(bf16))
                dscores.append((p * (tile(dp, t) - delta)).astype(bf16))
            ds = jnp.concatenate(dscores, 1)
            dqa_ref[...] += dot(ds, k_ref[w])
            dk_ref[w] += dot(q_t, ds)
            dv_ref[w] += dot(do_t, jnp.concatenate(probs, 1))

        def near_block(w, c):
            grad_block(w, False)
            return c

        lax.fori_loop(window.lo, window.last, near_block, 0)
        if final:
            grad_block(window.last, True)
            window.unstack(dq_ref, at, (dqa_ref[...] * scale).astype(bf16))
        else:
            window.unstack(dq_ref, at, dqa_ref[...])
        return carry

    lax.fori_loop(0, heads // STACK, step, 0)
    for w in range(count):
        dnear[w][0:dim] = (dk_ref[w] * scale).astype(bf16)
        dnear[w][dim : 2 * dim] = dv_ref[w].astype(bf16)
    if final:
        down[0:dim] = dk_ref[count] * scale
        down[dim : 2 * dim] = dv_ref[count]


def sum_kernel(half, down, older, *refs):
    *terms, dk_ref, dv_ref = refs
    total = down[...] + pieces(older, half)[-1][...].astype(f32)
    for term in terms:
        total = total + term[...].astype(f32)
    dim = dk_ref.shape[1]
    dk_ref[...] = total[0:dim].T.astype(bf16)
    dv_ref[...] = total[dim : 2 * dim].T.astype(bf16)


def call(kernel, near, args, outs, scratch, heads, name, plain=0):
    args = [*near, *args]
    held = [pltpu.with_memory_space_constraint(a, pltpu.VMEM) for a in args[: len(args) - plain]]
    args = held + args[len(held) :]
    vmem = pl.BlockSpec(memory_space=pltpu.VMEM)
    return pl.pallas_call(
        lambda *refs: kernel(len(near), heads, *refs),
        out_shape=outs,
        in_specs=[vmem] * len(args),
        out_specs=[vmem] * len(outs),
        scratch_shapes=scratch,
        compiler_params=pltpu.CompilerParams(vmem_limit_bytes=VMEM_BYTES),
        name=name,
    )(*args)


def attention_start(near, own, queries, dim):
    rows, width = queries.shape
    heads, blocks, stacked = width // dim, len(near) + 1, STACK * rows
    by_head = pltpu.VMEM((heads * rows, LANES), f32)
    outs = [pltpu.VMEM((rows, width), f32), by_head, by_head]
    scratch = [
        pltpu.VMEM((blocks, rows, dim), bf16),
        pltpu.VMEM((blocks, rows, 2 * dim), bf16),
        pltpu.VMEM((stacked, LANES), f32),
        pltpu.VMEM((stacked, LANES), f32),
        pltpu.VMEM((stacked, 2 * dim), f32),
        pltpu.VMEM((blocks, 8, rows), f32),
        pltpu.VMEM((stacked, LANES), f32),
    ]
    args = (own, queries)
    return call(start_kernel, near, args, outs, scratch, heads, "forward_near", plain=1)


def attention_far(far, own, queries, grad_out, state, dim):
    rows, width = queries.shape
    heads, blocks, stacked = width // dim, len(far), STACK * rows
    half = blocks - 1
    by_head = pltpu.VMEM((heads * rows, LANES), f32)
    outs = [jax.ShapeDtypeStruct((rows, width), bf16), pltpu.VMEM((rows, width), f32)]
    outs += [by_head, by_head, pltpu.VMEM((2 * dim, rows), bf16)]
    outs += [pltpu.VMEM((half * 2 * dim, rows), bf16)]
    scratch = [
        pltpu.VMEM((blocks, rows, dim), bf16),
        pltpu.VMEM((blocks, rows, 2 * dim), bf16),
        pltpu.VMEM((stacked, LANES), f32),
        pltpu.VMEM((stacked, LANES), f32),
        pltpu.VMEM((stacked, 2 * dim), f32),
        pltpu.VMEM((blocks + 1, 8, rows), f32),
        pltpu.VMEM((stacked, LANES), f32),
        pltpu.VMEM((blocks, stacked, rows), bf16),
        pltpu.VMEM((stacked, dim), f32),
        pltpu.VMEM((blocks, dim, rows), f32),
        pltpu.VMEM((blocks, dim, rows), f32),
    ]
    args = (own, queries, grad_out, *state)
    kernel = lambda count, heads, *refs: far_kernel(half, heads, *refs)
    return call(kernel, far, args, outs, scratch, heads, "attention_far")


def attention_back(final, near, own, queries, grad_out, dq, log_total, delta, dim):
    rows, width = queries.shape
    heads, blocks, stacked = width // dim, len(near) + int(final), STACK * rows
    if final:
        outs = [jax.ShapeDtypeStruct((rows, width), bf16)]
    else:
        outs = [pltpu.VMEM((rows, width), f32)]
    outs += [pltpu.VMEM((2 * dim, rows), bf16)] * len(near)
    if final:
        outs += [pltpu.VMEM((2 * dim, rows), f32)]
    scratch = [
        pltpu.VMEM((blocks, rows, dim), bf16),
        pltpu.VMEM((blocks, rows, dim), bf16),
        pltpu.VMEM((len(near) + 1, 8, rows), f32),
        pltpu.VMEM((stacked, LANES), f32),
        pltpu.VMEM((stacked, dim), f32),
        pltpu.VMEM((blocks, dim, rows), f32),
        pltpu.VMEM((blocks, dim, rows), f32),
    ]
    args = (own, queries, grad_out, dq, log_total, delta)
    name = "backward_final" if final else "backward_mid"
    return call(partial(back_kernel, final), near, args, outs, scratch, heads, name)


def sum_terms(down, older, half, terms, dim):
    rows = down.shape[1]
    out = jax.ShapeDtypeStruct((rows, dim), bf16)
    kernel = lambda count, heads, *refs: sum_kernel(half, *refs)
    return call(kernel, [down, older], terms, [out, out], [], 1, "sum_terms")


def shift(block, by):
    axes = ("outer", "inner")
    count = lax.axis_size(axes)
    return lax.ppermute(block, axes, [(i, (i + by) % count) for i in range(count)])


def on_device(queries, keys, values, grad_out, doc_ids):
    rows, dim = keys.shape
    reach = lax.axis_size("inner")
    docs = doc_ids.astype(bf16).reshape(rows // (2 * dim), 2 * dim)
    docs = jnp.pad(docs, ((0, DOC_ROWS - docs.shape[0]), (0, 0)))
    own = jnp.concatenate([jnp.concatenate([keys, values], 1), docs], 0)
    half = reach // 2
    behind = [shift(own, by) for by in range(reach, 0, -1)]
    far, near = behind[: half + 1], behind[half + 1 :]
    state = attention_start(near, own, queries, dim)
    attn_out, dq, log_total, delta, oldest_grads, older_grads = attention_far(
        far, own, queries, grad_out, state, dim
    )
    oldest_terms = shift(oldest_grads, -reach)
    older_terms = shift(older_grads, -half)
    dq, *grads = attention_back(
        False, near, own, queries, grad_out, dq, log_total, delta, dim
    )
    size = 2 * dim
    terms = [oldest_terms]
    for i, g in enumerate(grads):
        came = older_terms[i * size : (i + 1) * size]
        g = (g.astype(f32) + came.astype(f32)).astype(bf16)
        terms.append(shift(g, i + 1 - half))
    grad_q, own_grads = attention_back(
        True, [], own, queries, grad_out, dq, log_total, delta, dim
    )
    grad_k, grad_v = sum_terms(own_grads, older_terms, half, terms, dim)
    return (attn_out, grad_q, grad_k, grad_v)


def solution(mesh):
    rows = P(("outer", "inner"), None)
    return jax.shard_map(
        on_device,
        mesh=mesh,
        in_specs=(rows, rows, rows, rows, P(("outer", "inner"))),
        out_specs=(rows, rows, rows, rows),
        check_vma=False,
    )
```

```python
from functools import partial

import jax
import jax.numpy as jnp
from jax import lax
from jax.experimental import pallas as pl
from jax.experimental.pallas import tpu as pltpu
from jax.sharding import PartitionSpec as P

LOG2E = 1.4426950408889634
LOW = -1e30
HEADROOM = 64.0
LANES = 128
DOC_ROWS = 16
STACK = 4
VMEM_BYTES = 40 * 1024 * 1024
f32 = jnp.float32
bf16 = jnp.bfloat16
NN = (((1,), (0,)), ((), ()))
NT = (((1,), (1,)), ((), ()))


def dot(a, b, dims=NN):
    return lax.dot_general(a, b, dims, preferred_element_type=f32)


def tile(x, t):
    return x[:, t * LANES : (t + 1) * LANES]


def spread(column, like):
    return jnp.broadcast_to(column, like.shape)


class Window:
    def __init__(self, near, own, heads, q_ref, k_ref, v_ref, doc_ref, rowdoc_ref):
        rows, width = q_ref.shape
        self.rows, self.dim = rows, width // heads
        self.last = len(near)
        self.scale = self.dim ** (-0.5)
        self.k_ref, self.doc_ref, self.rowdoc_ref = k_ref, doc_ref, rowdoc_ref
        for w, ref in enumerate(near + [own]):
            if w < k_ref.shape[0]:
                k_ref[w] = ref[0:rows, 0 : self.dim]
                v_ref[w, :, 0 : self.dim] = ref[0:rows, self.dim : 2 * self.dim]
                if v_ref.shape[2] > self.dim:
                    v_ref[w, :, self.dim : 2 * self.dim] = jnp.ones((rows, self.dim), bf16)
            docs = ref[rows : rows + DOC_ROWS, :].astype(f32)
            for t in range(rows // LANES):
                part = docs[t // 2 : t // 2 + 1, (t % 2) * LANES : (t % 2 + 1) * LANES]
                doc_ref[w, 0:1, t * LANES : (t + 1) * LANES] = part
        first = jnp.broadcast_to(doc_ref[self.last, 0:1, 0:1], (1, LANES))
        spare = jnp.zeros((1, LANES), f32)
        for w in range(self.last):
            end = jnp.broadcast_to(doc_ref[w, 0:1, rows - 1 : rows], (1, LANES))
            spare = spare + jnp.where(end == first, 0.0, 1.0)
        self.lo = jnp.max(spare).astype(jnp.int32)
        row_docs = jnp.broadcast_to(doc_ref[self.last, 0:1, :], (LANES, rows)).T
        rowdoc_ref[...] = jnp.concatenate([row_docs] * STACK, 0)

    def masks(self, w, own_block):
        shape = self.rowdoc_ref.shape
        masks = []
        for t in range(self.rows // LANES):
            mask = self.rowdoc_ref[...] == self.doc_ref[w, 0:1, t * LANES : (t + 1) * LANES]
            if own_block:
                row = lax.rem(lax.broadcasted_iota(jnp.int32, shape, 0), self.rows)
                col = lax.broadcasted_iota(jnp.int32, shape, 1) + t * LANES
                mask = mask & (col <= row)
            masks.append(mask)
        return masks

    def scores(self, q, w, own_block):
        s = dot(q, self.k_ref[w], NT)
        return [
            jnp.where(mask, tile(s, t), LOW) for t, mask in enumerate(self.masks(w, own_block))
        ]

    def columns(self, at):
        return [
            pl.ds(pl.multiple_of((at * STACK + i) * self.dim, self.dim), self.dim)
            for i in range(STACK)
        ]

    def stacked_rows(self, at):
        count = STACK * self.rows
        return pl.ds(pl.multiple_of(at * count, count), count)

    def stack(self, ref, at):
        return jnp.concatenate([ref[:, c] for c in self.columns(at)], 0)

    def unstack(self, ref, at, value):
        for i, c in enumerate(self.columns(at)):
            ref[:, c] = value[i * self.rows : (i + 1) * self.rows]


def attend_near(window, q, own_block, m_ref, peak_ref, acc_ref, v_ref, p_ref, refill):
    scale = window.scale * LOG2E

    def attend(w, parts):
        m = m_ref[...]
        p = jnp.concatenate([jnp.exp2(s * scale - m) for s in parts], 1).astype(bf16)
        if p_ref is not None:
            p_ref[w] = p
        acc_ref[...] += dot(p, v_ref[w])

    if own_block:
        parts = window.scores(q, window.last, True)
        top = parts[0]
        for s in parts[1:]:
            top = jnp.maximum(top, s)
        refill(spread(jnp.max(top, axis=1, keepdims=True), top) * scale)
        attend(window.last, parts)
    else:
        refill(None)
    peak_ref[...] = jnp.full_like(peak_ref, LOW)

    def block(w, c):
        parts = window.scores(q, w, False)
        peak = peak_ref[...]
        for s in parts:
            peak = jnp.maximum(peak, s)
        peak_ref[...] = peak
        attend(w, parts)
        return c

    lax.fori_loop(window.lo, window.last, block, 0)
    excess = peak_ref[...] * scale - m_ref[...]

    @pl.when(jnp.max(excess) > HEADROOM)
    def _():
        peak = peak_ref[...]
        refill(jnp.maximum(m_ref[...], spread(jnp.max(peak, axis=1, keepdims=True), peak) * scale))

        def again(w, c):
            attend(w, window.scores(q, w, False))
            return c

        lax.fori_loop(window.lo, window.last, again, 0)
        if own_block:
            attend(window.last, window.scores(q, window.last, True))


def start_kernel(count, heads, *refs):
    refs = list(refs)
    near = [refs.pop(0) for _ in range(count)]
    own, q_ref, acc_out, m_out, l_out = [refs.pop(0) for _ in range(5)]
    k_ref, v_ref, m_ref, peak_ref, acc_ref, doc_ref, rowdoc_ref = refs
    window = Window(near, own, heads, q_ref, k_ref, v_ref, doc_ref, rowdoc_ref)
    dim = window.dim

    def step(at, carry):
        def refill(top):
            m_ref[...] = top
            acc_ref[...] = jnp.zeros_like(acc_ref)

        q = window.stack(q_ref, at)
        attend_near(window, q, True, m_ref, peak_ref, acc_ref, v_ref, None, refill)
        window.unstack(acc_out, at, acc_ref[:, 0:dim])
        m_out[window.stacked_rows(at)] = m_ref[...]
        l_out[window.stacked_rows(at)] = acc_ref[:, dim : 2 * dim]
        return carry

    lax.fori_loop(0, heads // STACK, step, 0)


def pieces(ref, count):
    rows = ref.shape[0] // count
    return [ref.at[pl.ds(i * rows, rows)] for i in range(count)]


def far_kernel(half, count, heads, *refs):
    refs = list(refs)
    back = half + 1
    near = [refs.pop(0) for _ in range(count)]
    near = near[-1:] + near[:-1]
    own, q_ref, do_ref, acc_in, m_in, l_in = [refs.pop(0) for _ in range(6)]
    out_ref, dq_ref, log_ref, delta_ref = [refs.pop(0) for _ in range(4)]
    dnear = [refs.pop(0), *pieces(refs.pop(0), half)]
    k_ref, v_ref, m_ref, peak_ref, acc_ref, doc_ref, rowdoc_ref, p_ref, dqa_ref, dk_ref, dv_ref = (
        refs
    )
    window = Window(near, own, heads, q_ref, k_ref, v_ref, doc_ref, rowdoc_ref)
    dim, tiles = window.dim, window.rows // LANES
    dk_ref[...] = jnp.zeros_like(dk_ref)
    dv_ref[...] = jnp.zeros_like(dv_ref)

    def step(at, carry):
        here = window.stacked_rows(at)

        def refill(top):
            old = m_in[here]
            m_ref[...] = old if top is None else top
            shrink = 1.0 if top is None else jnp.exp2(old - top)
            acc_ref[:, 0:dim] = window.stack(acc_in, at) * shrink
            acc_ref[:, dim : 2 * dim] = l_in[here] * shrink

        q = window.stack(q_ref, at)
        do = window.stack(do_ref, at)
        attend_near(window, q, False, m_ref, peak_ref, acc_ref, v_ref, p_ref, refill)
        total = acc_ref[:, dim : 2 * dim]
        inv = 1.0 / total
        out = (acc_ref[:, 0:dim] * inv).astype(bf16)
        dof = do.astype(f32)
        delta = jnp.sum(dof * out.astype(f32), axis=1, keepdims=True)
        log_ref[here] = m_ref[...] + jnp.log(total) * LOG2E
        delta_ref[here] = spread(delta, total)
        q_inv = (q.astype(f32) * inv).astype(bf16).T
        do_inv = (dof * inv).astype(bf16).T
        dqa_ref[...] = jnp.zeros_like(dqa_ref)

        def grad_block(w, c):
            dp = dot(do, v_ref[w, :, 0:dim], NT)
            delta = delta_ref[here]
            p = p_ref[w]
            parts = [
                (tile(p, t).astype(f32) * (tile(dp, t) - delta)).astype(bf16)
                for t in range(tiles)
            ]
            ds = jnp.concatenate(parts, 1)
            dqa_ref[...] += dot(ds, k_ref[w])
            dk_ref[w] += dot(q_inv, ds)
            dv_ref[w] += dot(do_inv, p)
            return c

        lax.fori_loop(window.lo, back, grad_block, 0)
        window.unstack(out_ref, at, out)
        window.unstack(dq_ref, at, dqa_ref[...] * inv)
        return carry

    lax.fori_loop(0, heads // STACK, step, 0)
    for w in range(back):
        dnear[w][0:dim] = (dk_ref[w] * window.scale).astype(bf16)
        dnear[w][dim : 2 * dim] = dv_ref[w].astype(bf16)


def back_kernel(final, count, heads, *refs):
    refs = list(refs)
    near = [refs.pop(0) for _ in range(count)]
    own, q_ref, do_ref, dq_in, log_ref, delta_ref = [refs.pop(0) for _ in range(6)]
    dq_ref = refs.pop(0)
    dnear = [refs.pop(0) for _ in range(count)]
    down = refs.pop(0) if final else None
    k_ref, v_ref, doc_ref, rowdoc_ref, dqa_ref, dk_ref, dv_ref = refs
    window = Window(near, own, heads, q_ref, k_ref, v_ref, doc_ref, rowdoc_ref)
    dim, scale = window.dim, window.scale
    dk_ref[...] = jnp.zeros_like(dk_ref)
    dv_ref[...] = jnp.zeros_like(dv_ref)

    def step(at, carry):
        here = window.stacked_rows(at)
        q = window.stack(q_ref, at)
        do = window.stack(do_ref, at)
        q_t = q.T
        do_t = do.T
        dqa_ref[...] = window.stack(dq_in, at)

        def grad_block(w, own_block):
            s = dot(q, k_ref[w], NT)
            dp = dot(do, v_ref[w], NT)
            top = log_ref[here]
            delta = delta_ref[here]
            probs = []
            dscores = []
            for t, mask in enumerate(window.masks(w, own_block)):
                p = jnp.where(mask, jnp.exp2(tile(s, t) * (scale * LOG2E) - top), 0.0)
                probs.append(p.astype(bf16))
                dscores.append((p * (tile(dp, t) - delta)).astype(bf16))
            ds = jnp.concatenate(dscores, 1)
            dqa_ref[...] += dot(ds, k_ref[w])
            dk_ref[w] += dot(q_t, ds)
            dv_ref[w] += dot(do_t, jnp.concatenate(probs, 1))

        def near_block(w, c):
            grad_block(w, False)
            return c

        lax.fori_loop(window.lo, window.last, near_block, 0)
        if final:
            grad_block(window.last, True)
            window.unstack(dq_ref, at, (dqa_ref[...] * scale).astype(bf16))
        else:
            window.unstack(dq_ref, at, dqa_ref[...])
        return carry

    lax.fori_loop(0, heads // STACK, step, 0)
    for w in range(count):
        dnear[w][0:dim] = (dk_ref[w] * scale).astype(bf16)
        dnear[w][dim : 2 * dim] = dv_ref[w].astype(bf16)
    if final:
        down[0:dim] = dk_ref[count] * scale
        down[dim : 2 * dim] = dv_ref[count]


def sum_kernel(half, down, older, *refs):
    *terms, dk_ref, dv_ref = refs
    total = down[...] + pieces(older, half)[-1][...].astype(f32)
    for term in terms:
        total = total + term[...].astype(f32)
    dim = dk_ref.shape[1]
    dk_ref[...] = total[0:dim].T.astype(bf16)
    dv_ref[...] = total[dim : 2 * dim].T.astype(bf16)


def call(kernel, near, args, outs, scratch, heads, name, plain=0):
    args = [*near, *args]
    held = [pltpu.with_memory_space_constraint(a, pltpu.VMEM) for a in args[: len(args) - plain]]
    args = held + args[len(held) :]
    vmem = pl.BlockSpec(memory_space=pltpu.VMEM)
    return pl.pallas_call(
        lambda *refs: kernel(len(near), heads, *refs),
        out_shape=outs,
        in_specs=[vmem] * len(args),
        out_specs=[vmem] * len(outs),
        scratch_shapes=scratch,
        compiler_params=pltpu.CompilerParams(vmem_limit_bytes=VMEM_BYTES),
        name=name,
    )(*args)


def attention_start(near, own, queries, dim):
    rows, width = queries.shape
    heads, blocks, stacked = width // dim, len(near) + 1, STACK * rows
    by_head = pltpu.VMEM((heads * rows, LANES), f32)
    outs = [pltpu.VMEM((rows, width), f32), by_head, by_head]
    scratch = [
        pltpu.VMEM((blocks, rows, dim), bf16),
        pltpu.VMEM((blocks, rows, 2 * dim), bf16),
        pltpu.VMEM((stacked, LANES), f32),
        pltpu.VMEM((stacked, LANES), f32),
        pltpu.VMEM((stacked, 2 * dim), f32),
        pltpu.VMEM((blocks, 8, rows), f32),
        pltpu.VMEM((stacked, LANES), f32),
    ]
    args = (own, queries)
    return call(start_kernel, near, args, outs, scratch, heads, "forward_near", plain=1)


def attention_far(far, half, own, queries, grad_out, state, dim):
    rows, width = queries.shape
    heads, blocks, stacked = width // dim, len(far), STACK * rows
    by_head = pltpu.VMEM((heads * rows, LANES), f32)
    outs = [jax.ShapeDtypeStruct((rows, width), bf16), pltpu.VMEM((rows, width), f32)]
    outs += [by_head, by_head, pltpu.VMEM((2 * dim, rows), bf16)]
    outs += [pltpu.VMEM((half * 2 * dim, rows), bf16)]
    scratch = [
        pltpu.VMEM((blocks, rows, dim), bf16),
        pltpu.VMEM((blocks, rows, 2 * dim), bf16),
        pltpu.VMEM((stacked, LANES), f32),
        pltpu.VMEM((stacked, LANES), f32),
        pltpu.VMEM((stacked, 2 * dim), f32),
        pltpu.VMEM((blocks + 1, 8, rows), f32),
        pltpu.VMEM((stacked, LANES), f32),
        pltpu.VMEM((blocks, stacked, rows), bf16),
        pltpu.VMEM((stacked, dim), f32),
        pltpu.VMEM((half + 1, dim, rows), f32),
        pltpu.VMEM((half + 1, dim, rows), f32),
    ]
    args = (own, queries, grad_out, *state)
    return call(partial(far_kernel, half), far[1:] + far[:1], args, outs, scratch, heads, "attention_far")


def attention_back(final, near, own, queries, grad_out, dq, log_total, delta, dim):
    rows, width = queries.shape
    heads, blocks, stacked = width // dim, len(near) + int(final), STACK * rows
    if final:
        outs = [jax.ShapeDtypeStruct((rows, width), bf16)]
    else:
        outs = [pltpu.VMEM((rows, width), f32)]
    outs += [pltpu.VMEM((2 * dim, rows), bf16)] * len(near)
    if final:
        outs += [pltpu.VMEM((2 * dim, rows), f32)]
    scratch = [
        pltpu.VMEM((blocks, rows, dim), bf16),
        pltpu.VMEM((blocks, rows, dim), bf16),
        pltpu.VMEM((len(near) + 1, 8, rows), f32),
        pltpu.VMEM((stacked, LANES), f32),
        pltpu.VMEM((stacked, dim), f32),
        pltpu.VMEM((blocks, dim, rows), f32),
        pltpu.VMEM((blocks, dim, rows), f32),
    ]
    args = (own, queries, grad_out, dq, log_total, delta)
    name = "backward_final" if final else "backward_mid"
    return call(partial(back_kernel, final), near, args, outs, scratch, heads, name)


def sum_terms(down, older, half, terms, dim):
    rows = down.shape[1]
    out = jax.ShapeDtypeStruct((rows, dim), bf16)
    kernel = lambda count, heads, *refs: sum_kernel(half, *refs)
    return call(kernel, [down, older], terms, [out, out], [], 1, "sum_terms")


def shift(block, by):
    axes = ("outer", "inner")
    count = lax.axis_size(axes)
    return lax.ppermute(block, axes, [(i, (i + by) % count) for i in range(count)])


def on_device(queries, keys, values, grad_out, doc_ids):
    rows, dim = keys.shape
    reach = lax.axis_size("inner")
    docs = doc_ids.astype(bf16).reshape(rows // (2 * dim), 2 * dim)
    docs = jnp.pad(docs, ((0, DOC_ROWS - docs.shape[0]), (0, 0)))
    own = jnp.concatenate([jnp.concatenate([keys, values], 1), docs], 0)
    half = reach // 2
    behind = [shift(own, by) for by in range(reach, 0, -1)]
    far, near = behind[: half + 2], behind[half + 1 :]
    state = attention_start(near[1:], own, queries, dim)
    attn_out, dq, log_total, delta, oldest_grads, older_grads = attention_far(
        far, half, own, queries, grad_out, state, dim
    )
    oldest_terms = shift(oldest_grads, -reach)
    older_terms = shift(older_grads, -half)
    dq, *grads = attention_back(
        False, near, own, queries, grad_out, dq, log_total, delta, dim
    )
    size = 2 * dim
    terms = [oldest_terms]
    for i, g in enumerate(grads):
        came = older_terms[i * size : (i + 1) * size]
        g = (g.astype(f32) + came.astype(f32)).astype(bf16)
        terms.append(shift(g, i + 1 - half))
    grad_q, own_grads = attention_back(
        True, [], own, queries, grad_out, dq, log_total, delta, dim
    )
    grad_k, grad_v = sum_terms(own_grads, older_terms, half, terms, dim)
    return (attn_out, grad_q, grad_k, grad_v)


def solution(mesh):
    rows = P(("outer", "inner"), None)
    return jax.shard_map(
        on_device,
        mesh=mesh,
        in_specs=(rows, rows, rows, rows, P(("outer", "inner"))),
        out_specs=(rows, rows, rows, rows),
        check_vma=False,
    )
```
